32 devices in a mesh: subj: 8 (over z, y), feat: 4 (over x, core).
Axes of the slice: x: 2, y: 2, z: 4, core: 2. Of those that a mesh axis runs over, the one named last changes fastest.
Arguments:
- visits: bfloat16 [64, 56, 10240], P('subj', None, 'feat'), may hold values from -6 to 6
- tile_pattern: int32 [64, 80], P('subj', 'feat'), may hold values 0 or 1
- counts: int32 [64], P('subj'), may hold values from 1 to 56, 1792 in all
- codes_t: bfloat16 [256, 10240], P('subj', 'feat'), may hold values from -0.0625 to 0.0625
- core: bfloat16 [256, 256], replicated, may hold values from -0.375 to 0.375
- patient_weights: float32 [64, 256], P('subj'), may hold values from 0.3 to 3
Outputs:
- code_mttkrp: float32 [256, 10240], P('subj', 'feat')
- patient_mttkrp: float32 [64, 256], P('subj')
The draws below stay inside these ranges and needn't reach their ends.
Inputs may be any that keep to these rules, and one draw needn't show every extreme that they name: `counts`: every patient has at least one visit; some patient has exactly 56.
All inputs are finite; a program needn't handle non-finite values. No bound on the sum of `tile_pattern` or of `counts` on one device may be relied on, other than what follows from the above.
Results may differ from the reference program's by a relative error of at most 0.0019.
Values may be sent and summed in bfloat16 or wider, within the bound.
No kernel may reach another device: no remote copies, remote signals or barrier semaphores. Data moves between devices by JAX's collectives and lax.ppermute only.
A program may use at most 64 MiB of HBM per device.

```python
import math
import jax
import jax.numpy as jnp
import numpy as np
from jax import lax

R = 256
J = 10240
TILE = 128
MAXV = 56
PAT_DEV = 8
NS_STEPS = 8
PATIENTS = 64
CODE_TILES = 80


def place_ends(entries, stream_key, least, high):
    longest = entries.shape.index(max(entries.shape))
    spots = []
    for shift in (0, 1):
        where = [jax.random.randint(jax.random.fold_in(stream_key, axis), (), 0, length) for axis, length in enumerate(entries.shape)]
        where[longest] = (where[longest] + shift) % entries.shape[longest]
        spots.append(tuple(where))
    return entries.at[spots[0]].set(least).at[spots[1]].set(high)


def block_scale(rng, extent, pieces, smallest, high):
    def one(axis_at, parts):
        steps = jax.random.uniform(jax.random.fold_in(jax.random.fold_in(rng, 6), axis_at), (parts,), jnp.float32, smallest / len(pieces), high / len(pieces))
        return jnp.repeat(jnp.exp(steps), extent[axis_at] // parts).reshape((-1,) + (1,) * (len(extent) - axis_at - 1))

    level = one(*pieces[0])
    for cut in pieces[1:]:
        level = level * one(*cut)
    return level


def split_up(number_of, total, most, skew):
    loads = [(1 << 20) // math.isqrt(standing ** skew) + 1 for standing in range(2, number_of + 1)]
    spare, given = total - most - (number_of - 1), [1] * (number_of - 1)
    while spare > 0:
        movable = [i for i in range(number_of - 1) if given[i] < most]
        mass, remaining = sum([loads[i] for i in movable]), spare
        for i in movable:
            more = min(most - given[i], max(1, remaining * loads[i] // mass), spare)
            given[i] = given[i] + more
            spare = spare - more
    return np.array([most] + given)


def uneven(key, number_of, total, reach, slope):
    if number_of == 2:
        one = jax.random.randint(key, (), max(1, total - reach), min(reach, total - 1) + 1)
        return jnp.stack([one, total - one])
    sizes = jnp.asarray(split_up(number_of, total, reach, slope), jnp.int32)
    pairs = (number_of - 1) // 2
    giver, sink = sizes[1:1 + 2 * pairs:2], sizes[2:2 + 2 * pairs:2]
    slack = jnp.minimum(giver - 1, reach - sink)
    moved = jax.random.randint(jax.random.fold_in(key, 1), (pairs,), 0, 1 << 20) % (slack + 1)
    sizes = sizes.at[1:1 + 2 * pairs:2].set(giver - moved).at[2:2 + 2 * pairs:2].set(sink + moved)
    return sizes[jax.random.permutation(jax.random.fold_in(key, 2), number_of)]


def bell_draw(stream_key, dims, spread, most, shards=(), kind=jnp.bfloat16):
    array = jax.random.normal(stream_key, dims, jnp.float32) * spread
    if len(shards) > 0:
        array = block_scale(stream_key, dims, shards, -0.22, 0.18) * array
    return jnp.clip(array, min=-most, max=most).astype(kind)


def setup_inputs(seed: int = 0) -> dict:
    arg_keys = jax.random.split(jax.random.key(seed), 7)
    visits = bell_draw(arg_keys[0], (PATIENTS, MAXV, J), 1.0, 6.0, ((0, 8), (2, 4)))
    tile_pattern = place_ends((jax.random.randint(arg_keys[1], (PATIENTS, CODE_TILES), 0, 2) < 1).astype(jnp.int32), jax.random.fold_in(arg_keys[1], 1), 0, 1)
    counts = uneven(arg_keys[2], PATIENTS, PATIENTS * MAXV // 2, MAXV, 1).astype(jnp.int32)
    codes_t = bell_draw(arg_keys[3], (R, J), J ** -0.5, 0.0625, ((0, 8), (1, 4)))
    core = bell_draw(arg_keys[4], (R, R), R ** -0.5, 0.375)
    patient_weights = jnp.clip(jnp.exp(math.log(3.0) - 2.3025851 * jax.random.uniform(arg_keys[5], (PATIENTS, R), jnp.float32) ** block_scale(arg_keys[5], (PATIENTS, R), ((0, 8),), -0.2, 0.2)), 0.3, 3.0)
    return dict(visits=visits, tile_pattern=tile_pattern, counts=counts, codes_t=codes_t, core=core, patient_weights=patient_weights)


def procrustes(projected, weights, core_f):
    scaled = projected * weights[:, None, :]
    target = jnp.einsum('pir,sr->pis', scaled, core_f, precision=lax.Precision.HIGHEST)
    total = lax.optimization_barrier(jnp.sum(target * target, axis=(1, 2)))
    rotation = target * lax.rsqrt(total + 1e-06)[:, None, None]
    for step in range(NS_STEPS):
        gram = jnp.einsum('pis,pks->pik', rotation, rotation, precision=lax.Precision.HIGHEST)
        rotation = 1.5 * rotation - 0.5 * jnp.einsum('pik,pks->pis', gram, rotation, precision=lax.Precision.HIGHEST)
    rotated = jnp.einsum('pis,sr->pir', rotation, core_f, precision=lax.Precision.HIGHEST)
    patient_rows = lax.optimization_barrier(jnp.sum(rotated * projected, axis=1))
    weighted = (rotated * weights[:, None, :]).astype(jnp.bfloat16)
    return (weighted, patient_rows)

def reference(visits, tile_pattern, counts, codes_t, core, patient_weights):
    core_f = core.astype(jnp.float32)
    blocks = PATIENTS // PAT_DEV
    visit_blocks = visits.reshape(blocks, PAT_DEV, MAXV, J)
    pattern_blocks = tile_pattern.reshape(blocks, PAT_DEV, CODE_TILES)
    count_blocks = counts.reshape(blocks, PAT_DEV)
    weight_blocks = patient_weights.reshape(blocks, PAT_DEV, R)

    def advance(total, block):
        values, pattern, lengths, weights = block
        live = (lax.broadcasted_iota(jnp.int32, (PAT_DEV, MAXV), 1) < lengths[:, None]).astype(jnp.int32)
        gate = (pattern[:, None, :, None] * live[:, :, None, None]).astype(jnp.bfloat16)
        masked = (values.reshape(PAT_DEV, MAXV, CODE_TILES, TILE) * gate).reshape(PAT_DEV * MAXV, J)
        projected = lax.dot_general(masked, codes_t, (((1,), (1,)), ((), ())), preferred_element_type=jnp.float32)
        weighted, patient_rows = procrustes(projected.reshape(PAT_DEV, MAXV, R), weights, core_f)
        term = lax.dot_general(weighted.reshape(PAT_DEV * MAXV, R), masked, (((0,), (0,)), ((), ())), preferred_element_type=jnp.float32)
        return (total + term, patient_rows)
    total, rows = lax.scan(advance, jnp.zeros((R, J), jnp.float32), (visit_blocks, pattern_blocks, count_blocks, weight_blocks))
    return (total, rows.reshape(PATIENTS, R))
```

```python
import functools

import jax
import jax.numpy as jnp
from jax import lax
from jax.experimental import pallas as pl
from jax.experimental.pallas import tpu as pltpu
from jax.sharding import PartitionSpec as P

NS_STEPS = 8
SLOT = 64
VMEM_BYTES = 32 * 1024 * 1024
CYCLE = (0, 2, 4, 6, 7, 5, 3, 1)
NT = (((1,), (1,)), ((), ()))
NN = (((1,), (0,)), ((), ()))


def dot(a, b, dims=NN):
    return lax.dot_general(a, b, dims, preferred_element_type=jnp.float32)


def split2(a):
    hi = a.astype(jnp.bfloat16)
    return hi, (a - hi.astype(jnp.float32)).astype(jnp.bfloat16)


def split3(a):
    hi = a.astype(jnp.bfloat16)
    rest = a - hi.astype(jnp.float32)
    mid = rest.astype(jnp.bfloat16)
    return hi, mid, (rest - mid.astype(jnp.float32)).astype(jnp.bfloat16)


def dot3(a, b, dims=NN):
    ah, al = a
    bh, bl = b
    return dot(ah, bh, dims) + (dot(ah, bl, dims) + dot(al, bh, dims))


def params():
    return pltpu.CompilerParams(vmem_limit_bytes=VMEM_BYTES)


def mask_body(counts_ref, gate_ref, visits_ref, masked_ref):
    k = pl.program_id(0)
    nvis, ncode = visits_ref.shape[1:]
    rows = lax.broadcasted_iota(jnp.int32, (nvis, 1), 0)
    live = (rows < counts_ref[k]).astype(jnp.bfloat16)
    vals = visits_ref[0] * (gate_ref[0] * live)
    masked_ref[...] = jnp.concatenate(
        [vals, jnp.zeros((SLOT - nvis, ncode), jnp.bfloat16)], 0
    )


def mask_visits(visits, tile_pattern, counts):
    npat, nvis, ncode = visits.shape
    gate = jnp.repeat(tile_pattern.astype(jnp.bfloat16), ncode // tile_pattern.shape[1], axis=1)
    return pl.pallas_call(
        mask_body,
        grid=(npat,),
        in_specs=[
            pl.BlockSpec(memory_space=pltpu.SMEM),
            pl.BlockSpec((1, 1, ncode), lambda k: (k, 0, 0)),
            pl.BlockSpec((1, nvis, ncode), lambda k: (k, 0, 0)),
        ],
        out_specs=pl.BlockSpec((SLOT, ncode), lambda k: (k, 0)),
        out_shape=jax.ShapeDtypeStruct((npat * SLOT, ncode), jnp.bfloat16),
        compiler_params=params(),
        cost_estimate=pl.CostEstimate(flops=0, bytes_accessed=6_000_000, transcendentals=0),
        name="mask_visits",
    )(counts, gate.reshape(npat, 1, ncode), visits)


def project_body(n, *refs):
    masked_ref, out_ref = refs[n], refs[n + 1]
    at = 0
    codes = jnp.concatenate([r[...] for r in refs[:n]], 0) if n > 1 else refs[0][...]
    out_ref[...] = dot(codes, masked_ref[...], NT)


def project(blocks, masked):
    rows = sum(b.shape[0] for b in blocks)
    return pl.pallas_call(
        functools.partial(project_body, len(blocks)),
        out_shape=jax.ShapeDtypeStruct((rows, masked.shape[0]), jnp.float32),
        compiler_params=params(),
        cost_estimate=pl.CostEstimate(
            flops=2 * rows * masked.size, bytes_accessed=2 * masked.size, transcendentals=0
        ),
        name="project",
    )(*blocks, masked)


def procrustes_body(block, counts, at_ref, *refs):
    n = len(counts)
    parts, (weights_ref, core_ref, coret_ref, wt_ref, rot_ref, proj_ref, projt, rott) = (
        refs[: 2 * n],
        refs[2 * n :],
    )
    npat, rank = weights_ref.shape
    slot = 0
    for g, blocks in enumerate(counts):
        for b in range(blocks):
            rows = slice(b * block, (b + 1) * block)
            base = pl.multiple_of(at_ref[slot] * block, block)
            projt[pl.ds(base, block), :] = parts[2 * g][rows, :] + parts[2 * g + 1][rows, :]
            slot += 1
    proj = projt[...].T
    proj_ref[...] = proj
    core, coret = core_ref[...], coret_ref[...]
    weights = weights_ref[...]
    wide = jnp.broadcast_to(weights[:, None, :], (npat, SLOT, rank)).reshape(npat * SLOT, rank)
    hi, mid, lo = split3(proj * wide)
    target = dot(hi, coret) + (dot(mid, coret) + dot(lo, coret))
    pair = 2 * SLOT
    row = lax.broadcasted_iota(jnp.int32, (pair, pair), 0) // SLOT
    col = lax.broadcasted_iota(jnp.int32, (pair, pair), 1) // SLOT
    same = row == col
    qs = []
    for p in range(npat // 2):
        two = target[p * pair : (p + 1) * pair].reshape(2, SLOT, rank)
        total = jnp.sum(jnp.sum(two * two, axis=1, keepdims=True), axis=2, keepdims=True)
        qs.append((two * lax.rsqrt(total + 1e-06)).reshape(pair, rank))
    for step in range(NS_STEPS):
        halves = [split2(q) for q in qs]
        grams = [jnp.where(same, dot3(h, h, NT), 0.0) for h in halves]
        prods = [dot3(split2(g), h) for g, h in zip(grams, halves)]
        qs = [1.5 * q - 0.5 * x for q, x in zip(qs, prods)]
    q = jnp.concatenate(qs, 0)
    hi, mid, lo = split3(q)
    rotated = dot(hi, core) + (dot(mid, core) + dot(lo, core))
    rot_ref[...] = rotated
    wt_ref[...] = (rotated * wide).T.astype(jnp.bfloat16)


def procrustes(groups, at, counts, weights, core, block):
    npat, rank = weights.shape
    rows = npat * SLOT
    flat = [a for pair in groups for a in pair]
    vmem = pl.BlockSpec(memory_space=pltpu.VMEM)
    return pl.pallas_call(
        functools.partial(procrustes_body, block, counts),
        in_specs=[pl.BlockSpec(memory_space=pltpu.SMEM)] + [vmem] * (len(flat) + 3),
        out_specs=[vmem] * 3,
        out_shape=[
            jax.ShapeDtypeStruct((rank, rows), jnp.bfloat16),
            jax.ShapeDtypeStruct((rows, rank), jnp.float32),
            jax.ShapeDtypeStruct((rows, rank), jnp.float32),
        ],
        scratch_shapes=[
            pltpu.VMEM((rank, rows), jnp.float32),
            pltpu.VMEM((8, 128), jnp.float32),
        ],
        compiler_params=params(),
        cost_estimate=pl.CostEstimate(
            flops=6 * 40 * rows * rank * 128, bytes_accessed=4_000_000, transcendentals=0
        ),
        name="procrustes",
    )(at, *flat, weights, core, core.T)


def rows_body(rot_ref, proj_ref, out_ref):
    npat, rank = out_ref.shape
    prod = rot_ref[...] * proj_ref[...]
    out_ref[...] = jnp.sum(prod.reshape(npat, SLOT, rank), axis=1)


def patient_rows(rot, proj, npat):
    return pl.pallas_call(
        rows_body,
        out_shape=jax.ShapeDtypeStruct((npat, rot.shape[1]), jnp.float32),
        compiler_params=params(),
        name="patient_rows",
    )(rot, proj)


def term_body(block, at_ref, wt_ref, masked_ref, send_ref, keep_ref):
    there = wt_ref[pl.ds(pl.multiple_of(at_ref[0] * block, block), block), :]
    here = wt_ref[pl.ds(pl.multiple_of(at_ref[1] * block, block), block), :]
    both = dot(jnp.concatenate([there, here], 0), masked_ref[...])
    send_ref[...] = both[:block].astype(send_ref.dtype)
    keep_ref[...] = both[block:]


def term(wt, masked, at, block, send_type):
    ncode = masked.shape[1]
    vmem = pl.BlockSpec(memory_space=pltpu.VMEM)
    return pl.pallas_call(
        functools.partial(term_body, block),
        in_specs=[pl.BlockSpec(memory_space=pltpu.SMEM), vmem, vmem],
        out_specs=[vmem, vmem],
        out_shape=[
            jax.ShapeDtypeStruct((block, ncode), send_type),
            jax.ShapeDtypeStruct((block, ncode), jnp.float32),
        ],
        compiler_params=params(),
        cost_estimate=pl.CostEstimate(
            flops=4 * block * masked.size, bytes_accessed=2 * masked.size, transcendentals=0
        ),
        name="term",
    )(at, wt, masked)


def flip(axis, size, bit):
    return functools.partial(
        lax.ppermute, axis_name=axis, perm=[(s, s ^ bit) for s in range(size)]
    )


def feat_sum(part):
    part = part + flip("feat", 4, 1)(part)
    return part, flip("feat", 4, 2)(part)


def per_device(visits, tile_pattern, counts, codes_t, core, patient_weights):
    npat = visits.shape[0]
    block = codes_t.shape[0]
    me = lax.axis_index("subj")
    cycle = jnp.array(CYCLE, jnp.int32)
    place = jnp.argmax(cycle == me).astype(jnp.int32)
    ahead = [(CYCLE[i], CYCLE[(i + 1) % 8]) for i in range(8)]
    back = [(d, s) for s, d in ahead]

    masked = mask_visits(visits, tile_pattern, counts)

    f, b = [codes_t], [codes_t]
    for _ in range(3):
        f.append(lax.ppermute(f[-1], "subj", ahead))
        b.append(lax.ppermute(b[-1], "subj", back))
    half = block // 2
    f4 = lax.ppermute(f[3][:half], "subj", ahead)
    b4 = lax.ppermute(b[3][half:], "subj", back)

    sets = [[codes_t, f[1], b[1], f[2], b[2]], [f[3], b[3]], [f4, b4]]
    offsets = jnp.array([0, -1, 1, -2, 2, -3, 3, 4], jnp.int32)
    at = cycle[(place + offsets) % 8]
    groups = [feat_sum(project(s, masked)) for s in sets]
    wt, rot, proj = procrustes(groups, at, (5, 2, 1), patient_weights, core, block)

    out = None
    for step in (3, 2, 1, 0):
        to = me ^ (2 * step)
        pick = jnp.stack([to ^ 1, to]).astype(jnp.int32)
        send, keep = term(wt, masked, pick, block, jnp.float32 if step == 0 else jnp.bfloat16)
        got = flip("subj", 8, 1)(send)
        both = keep + got.astype(jnp.float32)
        if step:
            both = flip("subj", 8, 2 * step)(both.astype(jnp.bfloat16)).astype(jnp.float32)
        out = both if out is None else out + both
    rows = patient_rows(rot, proj, npat)
    return out, rows


def per_device_any(visits, tile_pattern, counts, codes_t, core, patient_weights):
    npat = visits.shape[0]
    masked = mask_visits(visits, tile_pattern, counts)
    codes = lax.all_gather(codes_t, "subj", axis=0, tiled=True)
    part = lax.psum(project([codes], masked), "feat")
    rank = part.shape[0]
    groups = [(part, jnp.zeros_like(part))]
    wt, rot, proj = procrustes(
        groups, jnp.zeros((1,), jnp.int32), (1,), patient_weights, core, rank
    )
    half = rank // 2
    low, high = term(wt, masked, jnp.array([0, 1], jnp.int32), half, jnp.float32)
    whole = jnp.concatenate([low, high], 0)
    out = lax.psum_scatter(whole, "subj", scatter_dimension=0, tiled=True)
    return out, patient_rows(rot, proj, npat)


def solution(mesh):
    plan = per_device if (mesh.shape["subj"], mesh.shape["feat"]) == (8, 4) else per_device_any
    return jax.shard_map(
        plan,
        mesh=mesh,
        in_specs=(
            P("subj", None, "feat"),
            P("subj", "feat"),
            P("subj"),
            P("subj", "feat"),
            P(),
            P("subj", None),
        ),
        out_specs=(P("subj", "feat"), P("subj", None)),
        check_vma=False,
    )
```

```python
import functools

import jax
import jax.numpy as jnp
from jax import lax
from jax.experimental import pallas as pl
from jax.experimental.pallas import tpu as pltpu
from jax.sharding import PartitionSpec as P

NS_STEPS = 8
SLOT = 64
CYCLE = (0, 2, 4, 6, 7, 5, 3, 1)
AHEAD = [(CYCLE[i], CYCLE[(i + 1) % 8]) for i in range(8)]
BACK = [(d, s) for s, d in AHEAD]
NT = (((1,), (1,)), ((), ()))
NN = (((1,), (0,)), ((), ()))


def dot(a, b, dims=NN):
    return lax.dot_general(a, b, dims, preferred_element_type=jnp.float32)


def split2(a):
    hi = a.astype(jnp.bfloat16)
    return hi, (a - hi.astype(jnp.float32)).astype(jnp.bfloat16)


def split3(a):
    hi = a.astype(jnp.bfloat16)
    rest = a - hi.astype(jnp.float32)
    mid = rest.astype(jnp.bfloat16)
    return hi, mid, (rest - mid.astype(jnp.float32)).astype(jnp.bfloat16)


def dot3(a, b, dims=NN):
    ah, al = a
    bh, bl = b
    return dot(ah, bh, dims) + (dot(ah, bl, dims) + dot(al, bh, dims))


def params(mib):
    return pltpu.CompilerParams(vmem_limit_bytes=mib * 1024 * 1024)


def spot(order):
    me = lax.axis_index("subj")
    place = jnp.where(me % 2 == 0, me // 2, 7 - me // 2)
    at = (place + (order + 8)) % 8
    return jnp.where(at < 4, 2 * at, 15 - 2 * at)


def rows_of(index, block):
    return pl.ds(pl.multiple_of(index * block, block), block)


def mask_body(counts_ref, gate_ref, visits_ref, masked_ref):
    k = pl.program_id(0)
    nvis, ncode = visits_ref.shape[1:]
    rows = lax.broadcasted_iota(jnp.int32, (nvis, 1), 0)
    live = (rows < counts_ref[k]).astype(jnp.bfloat16)
    vals = visits_ref[0] * (gate_ref[0] * live)
    masked_ref[...] = jnp.concatenate(
        [vals, jnp.zeros((SLOT - nvis, ncode), jnp.bfloat16)], 0
    )


def mask_visits(visits, tile_pattern, counts):
    npat, nvis, ncode = visits.shape
    gate = jnp.repeat(tile_pattern.astype(jnp.bfloat16), ncode // tile_pattern.shape[1], axis=1)
    return pl.pallas_call(
        mask_body,
        grid=(npat,),
        in_specs=[
            pl.BlockSpec(memory_space=pltpu.SMEM),
            pl.BlockSpec((1, 1, ncode), lambda k: (k, 0, 0)),
            pl.BlockSpec((1, nvis, ncode), lambda k: (k, 0, 0)),
        ],
        out_specs=pl.BlockSpec((SLOT, ncode), lambda k: (k, 0)),
        out_shape=jax.ShapeDtypeStruct((npat * SLOT, ncode), jnp.bfloat16),
        compiler_params=params(4),
        cost_estimate=pl.CostEstimate(flops=0, bytes_accessed=6_000_000, transcendentals=0),
        name="mask_visits",
    )(counts, gate.reshape(npat, 1, ncode), visits)


def project_body(n, split, *refs):
    masked_ref, outs = refs[n], refs[n + 1 :]
    codes = jnp.concatenate([r[...] for r in refs[:n]], 0) if n > 1 else refs[0][...]
    both = dot(codes, masked_ref[...], NT)
    if not split:
        outs[0][...] = both
        return
    mine_ref, theirs_ref, whole = outs
    half = mine_ref.shape[0]
    whole[...] = both
    core = lax.axis_index("feat") % 2
    mine_ref[...] = whole[rows_of(core, half), :]
    theirs_ref[...] = whole[rows_of(1 - core, half), :]


def project(blocks, masked, split=False):
    rows = sum(b.shape[0] for b in blocks)
    cols = masked.shape[0]
    whole = jax.ShapeDtypeStruct((rows, cols), jnp.float32)
    part = jax.ShapeDtypeStruct((rows // 2, cols), jnp.float32)
    return pl.pallas_call(
        functools.partial(project_body, len(blocks), split),
        out_shape=(part, part) if split else whole,
        scratch_shapes=[pltpu.VMEM((rows, cols), jnp.float32)] if split else [],
        compiler_params=params(10),
        cost_estimate=pl.CostEstimate(
            flops=2 * rows * masked.size, bytes_accessed=2 * masked.size, transcendentals=0
        ),
        name="project",
    )(*blocks, masked)


def place_rows(projt, parts, block, plan):
    core = lax.axis_index("feat") % 2
    at = 0
    for blocks, split in plan:
        left, right = parts[at], parts[at + 1]
        at += 2
        if not split:
            for b, order in enumerate(blocks):
                rows = slice(b * block, (b + 1) * block)
                projt[rows_of(spot(order), block), :] = left[rows, :] + right[rows, :]
            continue
        half = block // 2
        count = len(blocks)
        bases = [spot(o) * 2 + h for o in blocks for h in (0, 1)]
        for u in range(count):
            rows = slice(u * half, (u + 1) * half)
            low, high = bases[u], bases[count + u]
            projt[rows_of(jnp.where(core == 0, low, high), half), :] = left[rows, :]
            projt[rows_of(jnp.where(core == 0, high, low), half), :] = right[rows, :]


def procrustes_body(block, plan, *refs):
    n = 2 * len(plan) if plan else 1
    parts, (weights_ref, core_ref, coret_ref, wt_ref, rot_ref, proj_ref, projt) = (
        refs[:n],
        refs[n:],
    )
    npat, rank = weights_ref.shape
    if plan:
        place_rows(projt, parts, block, plan)
    else:
        projt[...] = parts[0][...]
    proj = projt[...].T
    proj_ref[...] = proj
    core, coret = core_ref[...], coret_ref[...]
    weights = weights_ref[...]
    wide = jnp.broadcast_to(weights[:, None, :], (npat, SLOT, rank)).reshape(npat * SLOT, rank)
    hi, mid, lo = split3(proj * wide)
    target = dot(hi, coret) + (dot(mid, coret) + dot(lo, coret))
    pair = 2 * SLOT
    row = lax.broadcasted_iota(jnp.int32, (pair, pair), 0) // SLOT
    col = lax.broadcasted_iota(jnp.int32, (pair, pair), 1) // SLOT
    same = row == col
    qs = []
    for p in range(npat // 2):
        two = target[p * pair : (p + 1) * pair].reshape(2, SLOT, rank)
        total = jnp.sum(jnp.sum(two * two, axis=1, keepdims=True), axis=2, keepdims=True)
        qs.append((two * lax.rsqrt(total + 1e-06)).reshape(pair, rank))
    for step in range(NS_STEPS):
        halves = [split2(q) for q in qs]
        grams = [jnp.where(same, dot3(h, h, NT), 0.0) for h in halves]
        prods = [dot3(split2(g), h) for g, h in zip(grams, halves)]
        qs = [1.5 * q - 0.5 * x for q, x in zip(qs, prods)]
    q = jnp.concatenate(qs, 0)
    hi, mid, lo = split3(q)
    rotated = dot(hi, core) + (dot(mid, core) + dot(lo, core))
    rot_ref[...] = rotated
    wt_ref[...] = (rotated * wide).T.astype(jnp.bfloat16)


def procrustes(parts, plan, weights, core, block):
    npat, rank = weights.shape
    rows = npat * SLOT
    return pl.pallas_call(
        functools.partial(procrustes_body, block, plan),
        out_shape=[
            jax.ShapeDtypeStruct((rank, rows), jnp.bfloat16),
            jax.ShapeDtypeStruct((rows, rank), jnp.float32),
            jax.ShapeDtypeStruct((rows, rank), jnp.float32),
        ],
        scratch_shapes=[pltpu.VMEM((rank, rows), jnp.float32)],
        compiler_params=params(16),
        cost_estimate=pl.CostEstimate(
            flops=6 * 40 * rows * rank * 128, bytes_accessed=4_000_000, transcendentals=0
        ),
        name="procrustes",
    )(*parts, weights, core, core.T)


def rows_body(rot_ref, proj_ref, out_ref):
    npat, rank = out_ref.shape
    prod = rot_ref[...] * proj_ref[...]
    out_ref[...] = jnp.sum(prod.reshape(npat, SLOT, rank), axis=1)


def patient_rows(rot, proj, npat):
    return pl.pallas_call(
        rows_body,
        out_shape=jax.ShapeDtypeStruct((npat, rot.shape[1]), jnp.float32),
        compiler_params=params(4),
        name="patient_rows",
    )(rot, proj)


def term_body(block, picks, wt_ref, masked_ref, *out_refs):
    me = lax.axis_index("subj")
    flips = [f for pick in picks for f in pick]
    wt = jnp.concatenate([wt_ref[rows_of(me ^ f, block), :] for f in flips], 0)
    both = dot(wt, masked_ref[...])
    at = 0
    for out_ref in out_refs:
        rows = out_ref.shape[0]
        out_ref[...] = both[at : at + rows].astype(out_ref.dtype)
        at += rows


def term(wt, masked, block, picks, kind):
    ncode = masked.shape[1]
    rows = [len(pick) * block for pick in picks]
    return pl.pallas_call(
        functools.partial(term_body, block, picks),
        out_shape=[jax.ShapeDtypeStruct((r, ncode), kind) for r in rows],
        compiler_params=params(10),
        cost_estimate=pl.CostEstimate(
            flops=2 * sum(rows) * masked.size, bytes_accessed=2 * masked.size, transcendentals=0
        ),
        name="term",
    )(wt, masked)


def whole_term_body(wt_ref, masked_ref, out_ref):
    out_ref[...] = dot(wt_ref[...], masked_ref[...])


def whole_term(wt, masked):
    return pl.pallas_call(
        whole_term_body,
        out_shape=jax.ShapeDtypeStruct((wt.shape[0], masked.shape[1]), jnp.float32),
        compiler_params=params(16),
        name="whole_term",
    )(wt, masked)


def flip(axis, size, bit):
    return functools.partial(
        lax.ppermute, axis_name=axis, perm=[(s, s ^ bit) for s in range(size)]
    )


def feat_sum(blocks, masked):
    part = project(blocks, masked)
    part = part + flip("feat", 4, 1)(part)
    return part, flip("feat", 4, 2)(part)


def feat_sum_halves(blocks, masked):
    mine, theirs = project(blocks, masked, split=True)
    mine = mine + flip("feat", 4, 1)(theirs)
    mine = mine + flip("feat", 4, 2)(mine)
    return mine, flip("feat", 4, 1)(mine)


def per_device(visits, tile_pattern, counts, codes_t, core, patient_weights):
    npat = visits.shape[0]
    block = codes_t.shape[0]
    masked = mask_visits(visits, tile_pattern, counts)

    f, b = [codes_t], [codes_t]
    for _ in range(3):
        f.append(lax.ppermute(f[-1], "subj", AHEAD))
        b.append(lax.ppermute(b[-1], "subj", BACK))
    half = block // 2
    f4 = lax.ppermute(f[3][:half], "subj", AHEAD)
    b4 = lax.ppermute(b[3][half:], "subj", BACK)

    plan = (((0, -1, 1, -2, 2), True), ((-3, 3), True), ((4,), False))
    parts = [
        *feat_sum_halves([codes_t, f[1], b[1], f[2], b[2]], masked),
        *feat_sum_halves([f[3], b[3]], masked),
        *feat_sum([f4, b4], masked),
    ]
    wt, rot, proj = procrustes(parts, plan, patient_weights, core, block)

    y, z1, z2, z3 = (flip("subj", 8, bit) for bit in (1, 2, 4, 6))
    there3, there2, near = term(wt, masked, block, ((7,), (5,), (3, 2)), jnp.bfloat16)
    here3, here2, there0, here0 = term(
        wt, masked, block, ((6,), (4,), (1,), (0,)), jnp.float32
    )
    far3 = z3((here3 + y(there3).astype(jnp.float32)).astype(jnp.bfloat16))
    far2 = z2((here2 + y(there2).astype(jnp.float32)).astype(jnp.bfloat16))
    near = z1(near).astype(jnp.float32)
    other = y(there0 + near[:block])
    out = (here0 + near[block:]) + other + (far3.astype(jnp.float32) + far2.astype(jnp.float32))
    rows = patient_rows(rot, proj, npat)
    return out, rows


def per_device_any(visits, tile_pattern, counts, codes_t, core, patient_weights):
    npat = visits.shape[0]
    masked = mask_visits(visits, tile_pattern, counts)
    codes = lax.all_gather(codes_t, "subj", axis=0, tiled=True)
    part = lax.psum(project([codes], masked), "feat")
    wt, rot, proj = procrustes([part], None, patient_weights, core, part.shape[0])
    out = lax.psum_scatter(
        whole_term(wt, masked), "subj", scatter_dimension=0, tiled=True
    )
    return out, patient_rows(rot, proj, npat)


def solution(mesh):
    plan = per_device if (mesh.shape["subj"], mesh.shape["feat"]) == (8, 4) else per_device_any
    return jax.shard_map(
        plan,
        mesh=mesh,
        in_specs=(
            P("subj", None, "feat"),
            P("subj", "feat"),
            P("subj"),
            P("subj", "feat"),
            P(),
            P("subj", None),
        ),
        out_specs=(P("subj", "feat"), P("subj", None)),
        check_vma=False,
    )
```

```python
import functools

import jax
import jax.numpy as jnp
from jax import lax
from jax.experimental import pallas as pl
from jax.experimental.pallas import tpu as pltpu
from jax.sharding import PartitionSpec as P

NS_STEPS = 8
SLOT = 64
BF16, F32 = jnp.bfloat16, jnp.float32


def cost(us):
    return pl.CostEstimate(flops=0, bytes_accessed=int(us * 3.6e6), transcendentals=0)

CYCLE = (0, 2, 4, 6, 7, 5, 3, 1)
AHEAD = [(CYCLE[i], CYCLE[(i + 1) % 8]) for i in range(8)]
BACK = [(d, s) for s, d in AHEAD]
NT = (((1,), (1,)), ((), ()))
NN = (((1,), (0,)), ((), ()))


def dot(a, b, dims=NN):
    return lax.dot_general(a, b, dims, preferred_element_type=jnp.float32)


def split2(a):
    hi = a.astype(jnp.bfloat16)
    return hi, (a - hi.astype(jnp.float32)).astype(jnp.bfloat16)


def split3(a):
    hi = a.astype(jnp.bfloat16)
    rest = a - hi.astype(jnp.float32)
    mid = rest.astype(jnp.bfloat16)
    return hi, mid, (rest - mid.astype(jnp.float32)).astype(jnp.bfloat16)


def dot3(a, b, dims=NN):
    ah, al = a
    bh, bl = b
    return dot(ah, bh, dims) + (dot(ah, bl, dims) + dot(al, bh, dims))


def params(mib):
    return pltpu.CompilerParams(vmem_limit_bytes=mib * 1024 * 1024)


def spot(order):
    me = lax.axis_index("subj")
    place = jnp.where(me % 2 == 0, me // 2, 7 - me // 2)
    at = (place + (order + 8)) % 8
    return jnp.where(at < 4, 2 * at, 15 - 2 * at)


def rows_of(index, block):
    return pl.ds(pl.multiple_of(index * block, block), block)


def mask_body(counts_ref, gate_ref, visits_ref, masked_ref):
    k = pl.program_id(0)
    nvis, ncode = visits_ref.shape[1:]
    rows = lax.broadcasted_iota(jnp.int32, (nvis, 1), 0)
    live = (rows < counts_ref[k]).astype(jnp.bfloat16)
    vals = visits_ref[0] * (gate_ref[0] * live)
    masked_ref[...] = jnp.concatenate(
        [vals, jnp.zeros((SLOT - nvis, ncode), jnp.bfloat16)], 0
    )


def mask_visits(visits, tile_pattern, counts):
    npat, nvis, ncode = visits.shape
    gate = jnp.repeat(tile_pattern.astype(jnp.bfloat16), ncode // tile_pattern.shape[1], axis=1)
    return pl.pallas_call(
        mask_body,
        grid=(npat,),
        in_specs=[
            pl.BlockSpec(memory_space=pltpu.SMEM),
            pl.BlockSpec((1, 1, ncode), lambda k: (k, 0, 0)),
            pl.BlockSpec((1, nvis, ncode), lambda k: (k, 0, 0)),
        ],
        out_specs=pl.BlockSpec((SLOT, ncode), lambda k: (k, 0)),
        out_shape=jax.ShapeDtypeStruct((npat * SLOT, ncode), jnp.bfloat16),
        compiler_params=params(4),
        cost_estimate=cost(0),
        name="mask_visits",
    )(counts, gate.reshape(npat, 1, ncode), visits)


def project_body(n, split, *refs):
    masked_ref, outs = refs[n], refs[n + 1 :]
    codes = jnp.concatenate([r[...] for r in refs[:n]], 0) if n > 1 else refs[0][...]
    both = dot(codes, masked_ref[...], NT)
    if not split:
        outs[0][...] = both
        return
    mine_ref, theirs_ref, whole = outs
    half = mine_ref.shape[0]
    whole[...] = both
    core = lax.axis_index("feat") % 2
    mine_ref[...] = whole[rows_of(core, half), :]
    theirs_ref[...] = whole[rows_of(1 - core, half), :]


def project(blocks, masked, split=False):
    rows = sum(b.shape[0] for b in blocks)
    cols = masked.shape[0]
    whole = jax.ShapeDtypeStruct((rows, cols), jnp.float32)
    part = jax.ShapeDtypeStruct((rows // 2, cols), jnp.float32)
    return pl.pallas_call(
        functools.partial(project_body, len(blocks), split),
        out_shape=(part, part) if split else whole,
        scratch_shapes=[pltpu.VMEM((rows, cols), jnp.float32)] if split else [],
        compiler_params=params(10),
        cost_estimate=cost(0),
        name="project",
    )(*blocks, masked)


def place_rows(projt, parts, block, plan):
    core = lax.axis_index("feat") % 2
    at = 0
    for blocks, split in plan:
        left, right = parts[at], parts[at + 1]
        at += 2
        if not split:
            for b, order in enumerate(blocks):
                rows = slice(b * block, (b + 1) * block)
                projt[rows_of(spot(order), block), :] = left[rows, :] + right[rows, :]
            continue
        half = block // 2
        count = len(blocks)
        bases = [spot(o) * 2 + h for o in blocks for h in (0, 1)]
        for u in range(count):
            rows = slice(u * half, (u + 1) * half)
            low, high = bases[u], bases[count + u]
            projt[rows_of(jnp.where(core == 0, low, high), half), :] = left[rows, :]
            projt[rows_of(jnp.where(core == 0, high, low), half), :] = right[rows, :]


def procrustes_body(block, plan, *refs):
    n = 2 * len(plan) if plan else 1
    parts, (weights_ref, core_ref, coret_ref, wt_ref, rot_ref, proj_ref, projt) = (
        refs[:n],
        refs[n:],
    )
    npat, rank = weights_ref.shape
    if plan:
        place_rows(projt, parts, block, plan)
    else:
        projt[...] = parts[0][...]
    proj = projt[...].T
    proj_ref[...] = proj
    core, coret = core_ref[...], coret_ref[...]
    weights = weights_ref[...]
    wide = jnp.broadcast_to(weights[:, None, :], (npat, SLOT, rank)).reshape(npat * SLOT, rank)
    hi, mid, lo = split3(proj * wide)
    target = dot(hi, coret) + (dot(mid, coret) + dot(lo, coret))
    pair = 2 * SLOT
    row = lax.broadcasted_iota(jnp.int32, (pair, pair), 0) // SLOT
    col = lax.broadcasted_iota(jnp.int32, (pair, pair), 1) // SLOT
    same = row == col
    qs = []
    for p in range(npat // 2):
        two = target[p * pair : (p + 1) * pair].reshape(2, SLOT, rank)
        total = jnp.sum(jnp.sum(two * two, axis=1, keepdims=True), axis=2, keepdims=True)
        qs.append((two * lax.rsqrt(total + 1e-06)).reshape(pair, rank))
    for step in range(NS_STEPS):
        halves = [split2(q) for q in qs]
        grams = [jnp.where(same, dot3(h, h, NT), 0.0) for h in halves]
        prods = [dot3(split2(g), h) for g, h in zip(grams, halves)]
        qs = [1.5 * q - 0.5 * x for q, x in zip(qs, prods)]
    q = jnp.concatenate(qs, 0)
    hi, mid, lo = split3(q)
    rotated = dot(hi, core) + (dot(mid, core) + dot(lo, core))
    rot_ref[...] = rotated
    wt_ref[...] = (rotated * wide).T.astype(jnp.bfloat16)


def procrustes(parts, plan, weights, core, block):
    npat, rank = weights.shape
    rows = npat * SLOT
    return pl.pallas_call(
        functools.partial(procrustes_body, block, plan),
        out_shape=[
            jax.ShapeDtypeStruct((rank, rows), jnp.bfloat16),
            jax.ShapeDtypeStruct((rows, rank), jnp.float32),
            jax.ShapeDtypeStruct((rows, rank), jnp.float32),
        ],
        scratch_shapes=[pltpu.VMEM((rank, rows), jnp.float32)],
        compiler_params=params(16),
        cost_estimate=cost(0),
        name="procrustes",
    )(*parts, weights, core, core.T)


def rows_body(rot_ref, proj_ref, out_ref):
    npat, rank = out_ref.shape
    prod = rot_ref[...] * proj_ref[...]
    out_ref[...] = jnp.sum(prod.reshape(npat, SLOT, rank), axis=1)


def patient_rows(rot, proj, npat):
    return pl.pallas_call(
        rows_body,
        out_shape=jax.ShapeDtypeStruct((npat, rot.shape[1]), jnp.float32),
        compiler_params=params(4),
        name="patient_rows",
    )(rot, proj)


def term_body(block, picks, wt_ref, masked_ref, *out_refs):
    me = lax.axis_index("subj")
    flips = [f for pick in picks for f in pick]
    wt = jnp.concatenate([wt_ref[rows_of(me ^ f, block), :] for f in flips], 0)
    both = dot(wt, masked_ref[...])
    at = 0
    for out_ref in out_refs:
        rows = out_ref.shape[0]
        out_ref[...] = both[at : at + rows].astype(out_ref.dtype)
        at += rows


def term(wt, masked, block, picks, kinds):
    ncode = masked.shape[1]
    rows = [len(pick) * block for pick in picks]
    return pl.pallas_call(
        functools.partial(term_body, block, picks),
        out_shape=[jax.ShapeDtypeStruct((r, ncode), kind) for r, kind in zip(rows, kinds)],
        compiler_params=params(10),
        cost_estimate=cost(0),
        name="term",
    )(wt, masked)


def whole_term_body(wt_ref, masked_ref, out_ref):
    out_ref[...] = dot(wt_ref[...], masked_ref[...])


def whole_term(wt, masked):
    return pl.pallas_call(
        whole_term_body,
        out_shape=jax.ShapeDtypeStruct((wt.shape[0], masked.shape[1]), jnp.float32),
        compiler_params=params(16),
        name="whole_term",
    )(wt, masked)


def flip(axis, size, bit):
    return functools.partial(
        lax.ppermute, axis_name=axis, perm=[(s, s ^ bit) for s in range(size)]
    )


def tie(first, then):
    return lax.optimization_barrier((first, then))


def per_device(visits, tile_pattern, counts, codes_t, core, patient_weights):
    npat = visits.shape[0]
    block = codes_t.shape[0]
    half = block // 2
    to_core, to_x = flip("feat", 4, 1), flip("feat", 4, 2)

    def step(ahead, back):
        return lax.ppermute(ahead, "subj", AHEAD), lax.ppermute(back, "subj", BACK)

    masked = mask_visits(visits, tile_pattern, counts)
    one = step(codes_t, codes_t)
    masked, back = tie(masked, one[1])
    one = (one[0], back)
    two = step(*one)
    proj0 = project([codes_t, *one, *two], masked, split=True)
    core0 = proj0[0] + to_core(proj0[1])
    tot0 = core0 + to_x(core0)
    three = step(*two)
    four = step(three[0][:half], three[1][half:])
    proj1 = project([*three, *four], masked, split=True)
    core1 = proj1[0] + to_core(proj1[1])
    tot1 = core1 + to_x(core1)
    parts = [tot0, to_core(tot0), tot1, to_core(tot1)]
    plan = (((0, -1, 1, -2, 2), True), ((-3, 3, 4), True),)
    wt, rot, proj = procrustes(parts, plan, patient_weights, core, block)

    y, z1, z2, z3 = (flip("subj", 8, bit) for bit in (1, 2, 4, 6))
    there2, there3, near = term(wt, masked, block, ((5,), (7,), (3, 2)), (BF16, BF16, BF16))
    here2, here3, there0, here0 = term(
        wt, masked, block, ((4,), (6,), (1,), (0,)), (F32, F32, F32, F32)
    )
    got2, there3 = tie(y(there2), there3)
    far2 = z2((here2 + got2.astype(F32)).astype(BF16))
    far3 = z3((here3 + y(there3).astype(F32)).astype(BF16))
    near = z1(near).astype(F32)
    other = y(there0 + near[:block])
    out = (here0 + near[block:]) + other + (far3.astype(F32) + far2.astype(F32))
    rows = patient_rows(rot, proj, npat)
    return out, rows


def per_device_any(visits, tile_pattern, counts, codes_t, core, patient_weights):
    npat = visits.shape[0]
    masked = mask_visits(visits, tile_pattern, counts)
    codes = lax.all_gather(codes_t, "subj", axis=0, tiled=True)
    part = lax.psum(project([codes], masked), "feat")
    wt, rot, proj = procrustes([part], None, patient_weights, core, part.shape[0])
    out = lax.psum_scatter(
        whole_term(wt, masked), "subj", scatter_dimension=0, tiled=True
    )
    return out, patient_rows(rot, proj, npat)


def solution(mesh):
    plan = per_device if (mesh.shape["subj"], mesh.shape["feat"]) == (8, 4) else per_device_any
    return jax.shard_map(
        plan,
        mesh=mesh,
        in_specs=(
            P("subj", None, "feat"),
            P("subj", "feat"),
            P("subj"),
            P("subj", "feat"),
            P(),
            P("subj", None),
        ),
        out_specs=(P("subj", "feat"), P("subj", None)),
        check_vma=False,
    )
```

```python
import functools

import jax
import jax.numpy as jnp
from jax import lax
from jax.experimental import pallas as pl
from jax.experimental.pallas import tpu as pltpu
from jax.sharding import PartitionSpec as P

NS_STEPS = 8
SLOT = 64
BF16, F32 = jnp.bfloat16, jnp.float32
FIRST = ((5,), (7,), (3,), (2,))


def cost(us):
    return pl.CostEstimate(flops=0, bytes_accessed=int(us * 3.6e6), transcendentals=0)

CYCLE = (0, 2, 4, 6, 7, 5, 3, 1)
AHEAD = [(CYCLE[i], CYCLE[(i + 1) % 8]) for i in range(8)]
BACK = [(d, s) for s, d in AHEAD]
NT = (((1,), (1,)), ((), ()))
NN = (((1,), (0,)), ((), ()))


def dot(a, b, dims=NN):
    return lax.dot_general(a, b, dims, preferred_element_type=jnp.float32)


def split2(a):
    hi = a.astype(jnp.bfloat16)
    return hi, (a - hi.astype(jnp.float32)).astype(jnp.bfloat16)


def split3(a):
    hi = a.astype(jnp.bfloat16)
    rest = a - hi.astype(jnp.float32)
    mid = rest.astype(jnp.bfloat16)
    return hi, mid, (rest - mid.astype(jnp.float32)).astype(jnp.bfloat16)


def dot3(a, b, dims=NN):
    ah, al = a
    bh, bl = b
    return dot(ah, bh, dims) + (dot(ah, bl, dims) + dot(al, bh, dims))


def params(mib):
    return pltpu.CompilerParams(vmem_limit_bytes=mib * 1024 * 1024)


def spot(order):
    me = lax.axis_index("subj")
    place = jnp.where(me % 2 == 0, me // 2, 7 - me // 2)
    at = (place + (order + 8)) % 8
    return jnp.where(at < 4, 2 * at, 15 - 2 * at)


def rows_of(index, block):
    return pl.ds(pl.multiple_of(index * block, block), block)


def mask_body(counts_ref, gate_ref, visits_ref, masked_ref):
    k = pl.program_id(0)
    nvis, ncode = visits_ref.shape[1:]
    rows = lax.broadcasted_iota(jnp.int32, (nvis, 1), 0)
    live = (rows < counts_ref[k]).astype(jnp.bfloat16)
    vals = visits_ref[0] * (gate_ref[0] * live)
    masked_ref[...] = jnp.concatenate(
        [vals, jnp.zeros((SLOT - nvis, ncode), jnp.bfloat16)], 0
    )


def mask_visits(visits, tile_pattern, counts):
    npat, nvis, ncode = visits.shape
    gate = jnp.repeat(tile_pattern.astype(jnp.bfloat16), ncode // tile_pattern.shape[1], axis=1)
    return pl.pallas_call(
        mask_body,
        grid=(npat,),
        in_specs=[
            pl.BlockSpec(memory_space=pltpu.SMEM),
            pl.BlockSpec((1, 1, ncode), lambda k: (k, 0, 0)),
            pl.BlockSpec((1, nvis, ncode), lambda k: (k, 0, 0)),
        ],
        out_specs=pl.BlockSpec((SLOT, ncode), lambda k: (k, 0)),
        out_shape=jax.ShapeDtypeStruct((npat * SLOT, ncode), jnp.bfloat16),
        compiler_params=params(4),
        cost_estimate=cost(0),
        name="mask_visits",
    )(counts, gate.reshape(npat, 1, ncode), visits)


def project_body(n, split, *refs):
    masked_ref, outs = refs[n], refs[n + 1 :]
    codes = jnp.concatenate([r[...] for r in refs[:n]], 0) if n > 1 else refs[0][...]
    both = dot(codes, masked_ref[...], NT)
    if not split:
        outs[0][...] = both
        return
    mine_ref, theirs_ref, whole = outs
    half = mine_ref.shape[0]
    whole[...] = both
    core = lax.axis_index("feat") % 2
    mine_ref[...] = whole[rows_of(core, half), :]
    theirs_ref[...] = whole[rows_of(1 - core, half), :]


def project(blocks, masked, split=False):
    rows = sum(b.shape[0] for b in blocks)
    cols = masked.shape[0]
    whole = jax.ShapeDtypeStruct((rows, cols), jnp.float32)
    part = jax.ShapeDtypeStruct((rows // 2, cols), jnp.float32)
    return pl.pallas_call(
        functools.partial(project_body, len(blocks), split),
        out_shape=(part, part) if split else whole,
        scratch_shapes=[pltpu.VMEM((rows, cols), jnp.float32)] if split else [],
        compiler_params=params(10),
        cost_estimate=cost(0),
        name="project",
    )(*blocks, masked)


def place_rows(projt, parts, block, plan):
    core = lax.axis_index("feat") % 2
    at = 0
    for blocks, split in plan:
        left, right = parts[at], parts[at + 1]
        at += 2
        if not split:
            for b, order in enumerate(blocks):
                rows = slice(b * block, (b + 1) * block)
                projt[rows_of(spot(order), block), :] = left[rows, :] + right[rows, :]
            continue
        half = block // 2
        count = len(blocks)
        bases = [spot(o) * 2 + h for o in blocks for h in (0, 1)]
        for u in range(count):
            rows = slice(u * half, (u + 1) * half)
            low, high = bases[u], bases[count + u]
            projt[rows_of(jnp.where(core == 0, low, high), half), :] = left[rows, :]
            projt[rows_of(jnp.where(core == 0, high, low), half), :] = right[rows, :]


def procrustes_body(block, plan, *refs):
    n = 2 * len(plan) if plan else 1
    parts, (weights_ref, core_ref, coret_ref, *rest) = refs[:n], refs[n:]
    if plan:
        masked_ref, wt_ref, rot_ref, proj_ref, *sends, projt = rest
    else:
        wt_ref, rot_ref, proj_ref, projt = rest
    npat, rank = weights_ref.shape
    if plan:
        place_rows(projt, parts, block, plan)
    else:
        projt[...] = parts[0][...]
    proj = projt[...].T
    proj_ref[...] = proj
    core, coret = core_ref[...], coret_ref[...]
    weights = weights_ref[...]
    wide = jnp.broadcast_to(weights[:, None, :], (npat, SLOT, rank)).reshape(npat * SLOT, rank)
    hi, lo = split2(proj * wide)
    target = dot(hi, coret) + dot(lo, coret)
    pair = 2 * SLOT
    row = lax.broadcasted_iota(jnp.int32, (pair, pair), 0) // SLOT
    col = lax.broadcasted_iota(jnp.int32, (pair, pair), 1) // SLOT
    same = row == col
    qs = []
    for p in range(npat // 2):
        two = target[p * pair : (p + 1) * pair].reshape(2, SLOT, rank)
        total = jnp.sum(jnp.sum(two * two, axis=1, keepdims=True), axis=2, keepdims=True)
        qs.append((two * lax.rsqrt(total + 1e-06)).reshape(pair, rank))
    for step in range(NS_STEPS):
        halves = [split2(q) for q in qs]
        stacks = [jnp.concatenate(h, 0) for h in halves]
        wides = [dot(k, k, NT) for k in stacks]
        grams = [w[:pair, :pair] + (w[:pair, pair:] + w[pair:, :pair]) for w in wides]
        grams = [split2(jnp.where(same, g, 0.0)) for g in grams]
        prods = [
            dot(jnp.concatenate([g[0], g[0]], 1), k) + dot(g[1], h[0])
            for g, h, k in zip(grams, halves, stacks)
        ]
        qs = [1.5 * q - 0.5 * x for q, x in zip(qs, prods)]
    q = jnp.concatenate(qs, 0)
    hi, lo = split2(q)
    rotated = dot(hi, core) + dot(lo, core)
    rot_ref[...] = rotated
    wt_ref[...] = (rotated * wide).T.astype(jnp.bfloat16)
    if plan:
        term_body(block, FIRST, wt_ref, masked_ref, *sends)


def procrustes(parts, plan, weights, core, block, masked=None):
    npat, rank = weights.shape
    rows = npat * SLOT
    sends = [] if masked is None else [
        jax.ShapeDtypeStruct((len(pick) * block, masked.shape[1]), BF16) for pick in FIRST
    ]
    return pl.pallas_call(
        functools.partial(procrustes_body, block, plan),
        out_shape=[
            jax.ShapeDtypeStruct((rank, rows), jnp.bfloat16),
            jax.ShapeDtypeStruct((rows, rank), jnp.float32),
            jax.ShapeDtypeStruct((rows, rank), jnp.float32),
            *sends,
        ],
        scratch_shapes=[pltpu.VMEM((rank, rows), jnp.float32)],
        compiler_params=params(16),
        cost_estimate=cost(4.8),
        name="procrustes",
    )(*parts, weights, core, core.T, *([] if masked is None else [masked]))


def rows_body(rot_ref, proj_ref, out_ref):
    npat, rank = out_ref.shape
    prod = rot_ref[...] * proj_ref[...]
    out_ref[...] = jnp.sum(prod.reshape(npat, SLOT, rank), axis=1)


def patient_rows(rot, proj, npat):
    return pl.pallas_call(
        rows_body,
        out_shape=jax.ShapeDtypeStruct((npat, rot.shape[1]), jnp.float32),
        compiler_params=params(4),
        name="patient_rows",
    )(rot, proj)


def term_body(block, picks, wt_ref, masked_ref, *out_refs):
    me = lax.axis_index("subj")
    flips = [f for pick in picks for f in pick]
    wt = jnp.concatenate([wt_ref[rows_of(me ^ f, block), :] for f in flips], 0)
    both = dot(wt, masked_ref[...])
    at = 0
    for out_ref in out_refs:
        rows = out_ref.shape[0]
        out_ref[...] = both[at : at + rows].astype(out_ref.dtype)
        at += rows


def term(wt, masked, block, picks, kinds):
    ncode = masked.shape[1]
    rows = [len(pick) * block for pick in picks]
    return pl.pallas_call(
        functools.partial(term_body, block, picks),
        out_shape=[jax.ShapeDtypeStruct((r, ncode), kind) for r, kind in zip(rows, kinds)],
        compiler_params=params(10),
        cost_estimate=cost(0),
        name="term",
    )(wt, masked)


def whole_term_body(wt_ref, masked_ref, out_ref):
    out_ref[...] = dot(wt_ref[...], masked_ref[...])


def whole_term(wt, masked):
    return pl.pallas_call(
        whole_term_body,
        out_shape=jax.ShapeDtypeStruct((wt.shape[0], masked.shape[1]), jnp.float32),
        compiler_params=params(16),
        name="whole_term",
    )(wt, masked)


def flip(axis, size, bit):
    return functools.partial(
        lax.ppermute, axis_name=axis, perm=[(s, s ^ bit) for s in range(size)]
    )


def tie(first, then):
    return lax.optimization_barrier((first, then))


def per_device(visits, tile_pattern, counts, codes_t, core, patient_weights):
    npat = visits.shape[0]
    block = codes_t.shape[0]
    half = block // 2
    to_core, to_x = flip("feat", 4, 1), flip("feat", 4, 2)

    def step(ahead, back):
        return lax.ppermute(ahead, "subj", AHEAD), lax.ppermute(back, "subj", BACK)

    masked = mask_visits(visits, tile_pattern, counts)
    one = step(codes_t, codes_t)
    masked, back = tie(masked, one[1])
    one = (one[0], back)
    two = step(*one)
    proj0 = project([codes_t, *one, *two], masked, split=True)
    core0 = proj0[0] + to_core(proj0[1])
    tot0 = core0 + to_x(core0)
    three = step(*two)
    four = step(three[0][:half], three[1][half:])
    proj1 = project([*three, *four], masked, split=True)
    core1 = proj1[0] + to_core(proj1[1])
    tot1 = core1 + to_x(core1)
    parts = [tot0, to_core(tot0), tot1, to_core(tot1)]
    plan = (((0, -1, 1, -2, 2), True), ((-3, 3, 4), True),)
    wt, rot, proj, there2, there3, near, own = procrustes(
        parts, plan, patient_weights, core, block, masked
    )

    y, z1, z2, z3 = (flip("subj", 8, bit) for bit in (1, 2, 4, 6))
    here2, here3, there0, here0 = term(
        wt, masked, block, ((4,), (6,), (1,), (0,)), (F32, F32, F32, F32)
    )
    got2, own = tie(y(there2), own)
    far2 = z2((here2 + got2.astype(F32)).astype(BF16)).astype(F32)
    got3 = y(there3)
    far3 = z3((here3 + got3.astype(F32)).astype(BF16)).astype(F32)
    other = there0 + z1(near).astype(F32)
    other = jnp.concatenate([y(p) for p in jnp.split(other, 2, axis=0)], 0)
    own = z1(own).astype(F32)
    out = (((here0 + own) + far2) + far3) + other
    rows = patient_rows(rot, proj, npat)
    return out, rows


def per_device_any(visits, tile_pattern, counts, codes_t, core, patient_weights):
    npat = visits.shape[0]
    masked = mask_visits(visits, tile_pattern, counts)
    codes = lax.all_gather(codes_t, "subj", axis=0, tiled=True)
    part = lax.psum(project([codes], masked), "feat")
    wt, rot, proj = procrustes([part], None, patient_weights, core, part.shape[0])
    out = lax.psum_scatter(
        whole_term(wt, masked), "subj", scatter_dimension=0, tiled=True
    )
    return out, patient_rows(rot, proj, npat)


def solution(mesh):
    plan = per_device if (mesh.shape["subj"], mesh.shape["feat"]) == (8, 4) else per_device_any
    return jax.shard_map(
        plan,
        mesh=mesh,
        in_specs=(
            P("subj", None, "feat"),
            P("subj", "feat"),
            P("subj"),
            P("subj", "feat"),
            P(),
            P("subj", None),
        ),
        out_specs=(P("subj", "feat"), P("subj", None)),
        check_vma=False,
    )
```

```python
import functools

import jax
import jax.numpy as jnp
from jax import lax
from jax.experimental import pallas as pl
from jax.experimental.pallas import tpu as pltpu
from jax.sharding import PartitionSpec as P

NS_STEPS = 8
SLOT = 64
BF16, F32 = jnp.bfloat16, jnp.float32
FIRST = ((5,), (7,), (3,), (2,))


def cost(us):
    return pl.CostEstimate(flops=0, bytes_accessed=int(us * 3.6e6), transcendentals=0)

CYCLE = (0, 2, 4, 6, 7, 5, 3, 1)
AHEAD = [(CYCLE[i], CYCLE[(i + 1) % 8]) for i in range(8)]
BACK = [(d, s) for s, d in AHEAD]
NT = (((1,), (1,)), ((), ()))
NN = (((1,), (0,)), ((), ()))


def dot(a, b, dims=NN):
    return lax.dot_general(a, b, dims, preferred_element_type=jnp.float32)


def split2(a):
    hi = a.astype(jnp.bfloat16)
    return hi, (a - hi.astype(jnp.float32)).astype(jnp.bfloat16)


def split3(a):
    hi = a.astype(jnp.bfloat16)
    rest = a - hi.astype(jnp.float32)
    mid = rest.astype(jnp.bfloat16)
    return hi, mid, (rest - mid.astype(jnp.float32)).astype(jnp.bfloat16)


def dot3(a, b, dims=NN):
    ah, al = a
    bh, bl = b
    return dot(ah, bh, dims) + (dot(ah, bl, dims) + dot(al, bh, dims))


def params(mib):
    return pltpu.CompilerParams(vmem_limit_bytes=mib * 1024 * 1024)


def spot(order):
    me = lax.axis_index("subj")
    place = jnp.where(me % 2 == 0, me // 2, 7 - me // 2)
    at = (place + (order + 8)) % 8
    return jnp.where(at < 4, 2 * at, 15 - 2 * at)


def rows_of(index, block):
    return pl.ds(pl.multiple_of(index * block, block), block)


def mask_body(counts_ref, gate_ref, visits_ref, masked_ref):
    k = pl.program_id(0)
    nvis, ncode = visits_ref.shape[1:]
    rows = lax.broadcasted_iota(jnp.int32, (nvis, 1), 0)
    live = (rows < counts_ref[k]).astype(jnp.bfloat16)
    vals = visits_ref[0] * (gate_ref[0] * live)
    masked_ref[...] = jnp.concatenate(
        [vals, jnp.zeros((SLOT - nvis, ncode), jnp.bfloat16)], 0
    )


def mask_visits(visits, tile_pattern, counts):
    npat, nvis, ncode = visits.shape
    gate = jnp.repeat(tile_pattern.astype(jnp.bfloat16), ncode // tile_pattern.shape[1], axis=1)
    return pl.pallas_call(
        mask_body,
        grid=(npat,),
        in_specs=[
            pl.BlockSpec(memory_space=pltpu.SMEM),
            pl.BlockSpec((1, 1, ncode), lambda k: (k, 0, 0)),
            pl.BlockSpec((1, nvis, ncode), lambda k: (k, 0, 0)),
        ],
        out_specs=pl.BlockSpec((SLOT, ncode), lambda k: (k, 0)),
        out_shape=jax.ShapeDtypeStruct((npat * SLOT, ncode), jnp.bfloat16),
        compiler_params=params(4),
        cost_estimate=cost(0),
        name="mask_visits",
    )(counts, gate.reshape(npat, 1, ncode), visits)


def project_body(n, cuts, *refs):
    masked_ref, outs = refs[n], refs[n + 1 :]
    codes = jnp.concatenate([r[...] for r in refs[:n]], 0) if n > 1 else refs[0][...]
    both = dot(codes, masked_ref[...], NT)
    if not cuts:
        outs[0][...] = both
        return
    *outs, whole = outs
    whole[...] = both
    core = lax.axis_index("feat") % 2
    for who, pieces in ((core, outs[: len(cuts)]), (1 - core, outs[len(cuts) :])):
        at = who * sum(cuts)
        for piece, rows in zip(pieces, cuts):
            piece[...] = whole[pl.ds(pl.multiple_of(at, 8), rows), :]
            at = at + rows


def project(blocks, masked, cuts=()):
    rows = sum(b.shape[0] for b in blocks)
    cols = masked.shape[0]
    shapes = [jax.ShapeDtypeStruct((r, cols), F32) for r in (tuple(cuts) * 2 or (rows,))]
    outs = pl.pallas_call(
        functools.partial(project_body, len(blocks), cuts),
        out_shape=shapes,
        scratch_shapes=[pltpu.VMEM((rows, cols), F32)] if cuts else [],
        compiler_params=params(10),
        cost_estimate=cost(0),
        name="project",
    )(*blocks, masked)
    return (outs[: len(cuts)], outs[len(cuts) :]) if cuts else outs[0]


def place_rows(projt, parts, block, plan):
    core = lax.axis_index("feat") % 2
    parts = list(parts)
    for orders, cuts, back in plan:
        if not cuts:
            left, right = parts.pop(0), parts.pop(0)
            for b, order in enumerate(orders):
                rows = slice(b * block, (b + 1) * block)
                projt[rows_of(spot(order), block), :] = left[rows, :] + right[rows, :]
            continue
        half = block // 2
        bases = [spot(o) * 2 + h for o in orders for h in (0, 1)]
        for who, sizes in ((core, cuts), (1 - core, back)):
            at = 0
            for rows in sizes:
                piece = parts.pop(0)
                for u in range(rows // half):
                    base = jnp.where(who == 0, bases[at], bases[len(orders) + at])
                    projt[rows_of(base, half), :] = piece[u * half : (u + 1) * half, :]
                    at += 1


def procrustes_body(block, plan, *refs):
    n = sum(len(cuts) + len(back) or 2 for _, cuts, back in plan) if plan else 1
    parts, (weights_ref, core_ref, *rest) = refs[:n], refs[n:]
    if plan:
        masked_ref, wt_ref, rot_ref, proj_ref, *sends, projt = rest
    else:
        wt_ref, rot_ref, proj_ref, projt = rest
    npat, rank = weights_ref.shape
    if plan:
        place_rows(projt, parts, block, plan)
    else:
        projt[...] = parts[0][...]
    proj = projt[...].T
    proj_ref[...] = proj
    core = core_ref[...]
    weights = weights_ref[...]
    wide = jnp.broadcast_to(weights[:, None, :], (npat, SLOT, rank)).reshape(npat * SLOT, rank)
    hi, lo = split2(proj * wide)
    target = dot(hi, core, NT) + dot(lo, core, NT)
    pair = 2 * SLOT
    row = lax.broadcasted_iota(jnp.int32, (pair, pair), 0) // SLOT
    col = lax.broadcasted_iota(jnp.int32, (pair, pair), 1) // SLOT
    same = row == col
    qs = []
    for p in range(npat // 2):
        two = target[p * pair : (p + 1) * pair].reshape(2, SLOT, rank)
        total = jnp.sum(jnp.sum(two * two, axis=1, keepdims=True), axis=2, keepdims=True)
        qs.append((two * lax.rsqrt(total + 1e-06)).reshape(pair, rank))
    for step in range(NS_STEPS):
        halves = [split2(q) for q in qs]
        stacks = [jnp.concatenate(h, 0) for h in halves]
        wides = [dot(k, k, NT) for k in stacks]
        grams = [w[:pair, :pair] + (w[:pair, pair:] + w[pair:, :pair]) for w in wides]
        grams = [split2(jnp.where(same, g, 0.0)) for g in grams]
        prods = [
            dot(jnp.concatenate([g[0], g[0]], 1), k) + dot(g[1], h[0])
            for g, h, k in zip(grams, halves, stacks)
        ]
        qs = [1.5 * q - 0.5 * x for q, x in zip(qs, prods)]
    q = jnp.concatenate(qs, 0)
    hi, lo = split2(q)
    rotated = dot(hi, core) + dot(lo, core)
    rot_ref[...] = rotated
    wt_ref[...] = (rotated * wide).T.astype(jnp.bfloat16)
    if plan:
        term_body(block, FIRST, wt_ref, masked_ref, *sends)


def procrustes(parts, plan, weights, core, block, masked=None):
    npat, rank = weights.shape
    rows = npat * SLOT
    sends = [] if masked is None else [
        jax.ShapeDtypeStruct((len(pick) * block, masked.shape[1]), BF16) for pick in FIRST
    ]
    return pl.pallas_call(
        functools.partial(procrustes_body, block, plan),
        out_shape=[
            jax.ShapeDtypeStruct((rank, rows), jnp.bfloat16),
            jax.ShapeDtypeStruct((rows, rank), jnp.float32),
            jax.ShapeDtypeStruct((rows, rank), jnp.float32),
            *sends,
        ],
        scratch_shapes=[pltpu.VMEM((rank, rows), jnp.float32)],
        compiler_params=params(16),
        cost_estimate=cost(4.8),
        name="procrustes",
    )(*parts, weights, core, *([] if masked is None else [masked]))


def rows_body(rot_ref, proj_ref, out_ref):
    npat, rank = out_ref.shape
    prod = rot_ref[...] * proj_ref[...]
    out_ref[...] = jnp.sum(prod.reshape(npat, SLOT, rank), axis=1)


def patient_rows(rot, proj, npat):
    return pl.pallas_call(
        rows_body,
        out_shape=jax.ShapeDtypeStruct((npat, rot.shape[1]), jnp.float32),
        compiler_params=params(4),
        name="patient_rows",
    )(rot, proj)


def term_body(block, picks, wt_ref, masked_ref, *out_refs):
    me = lax.axis_index("subj")
    flips = [f for pick in picks for f in pick]
    wt = jnp.concatenate([wt_ref[rows_of(me ^ f, block), :] for f in flips], 0)
    both = dot(wt, masked_ref[...])
    at = 0
    for out_ref in out_refs:
        rows = out_ref.shape[0]
        out_ref[...] = both[at : at + rows].astype(out_ref.dtype)
        at += rows


def term(wt, masked, block, picks, kinds):
    ncode = masked.shape[1]
    rows = [len(pick) * block for pick in picks]
    return pl.pallas_call(
        functools.partial(term_body, block, picks),
        out_shape=[jax.ShapeDtypeStruct((r, ncode), kind) for r, kind in zip(rows, kinds)],
        compiler_params=params(10),
        cost_estimate=cost(0),
        name="term",
    )(wt, masked)


def whole_term_body(wt_ref, masked_ref, out_ref):
    out_ref[...] = dot(wt_ref[...], masked_ref[...])


def whole_term(wt, masked):
    return pl.pallas_call(
        whole_term_body,
        out_shape=jax.ShapeDtypeStruct((wt.shape[0], masked.shape[1]), jnp.float32),
        compiler_params=params(16),
        name="whole_term",
    )(wt, masked)


def flip(axis, size, bit):
    return functools.partial(
        lax.ppermute, axis_name=axis, perm=[(s, s ^ bit) for s in range(size)]
    )


def tie(first, then):
    return lax.optimization_barrier((first, then))


def cut(a, rows):
    return jnp.split(a, a.shape[0] // rows, axis=0)


def per_device(visits, tile_pattern, counts, codes_t, core, patient_weights):
    npat = visits.shape[0]
    block = codes_t.shape[0]
    half = block // 2
    to_core, to_x = flip("feat", 4, 1), flip("feat", 4, 2)

    def step(ahead, back):
        return lax.ppermute(ahead, "subj", AHEAD), lax.ppermute(back, "subj", BACK)

    masked = mask_visits(visits, tile_pattern, counts)
    one = step(codes_t, codes_t)
    masked, back = tie(masked, one[1])
    one = (one[0], back)
    two = step(*one)
    three = step(*two)
    four = (lax.ppermute(three[1], "subj", BACK),)
    cuts0 = (5 * half,)
    sums0 = [m + to_core(t) for m, t in zip(*project([codes_t, *one, *two], masked, cuts0))]
    from0 = [to_x(s) for s in sums0]
    cuts1 = (2 * half,)
    sums1 = [m + to_core(t) for m, t in zip(*project([*three], masked, cuts1))]
    from1 = [to_x(s) for s in sums1]
    sums2 = project([*four], masked)
    sums2 = sums2 + to_core(sums2)
    sums2, from1 = tie(sums2, from1)
    sums0 = [s + f for s, f in zip(sums0, from0)]
    sums1 = [s + f for s, f in zip(sums1, from1)]
    back0 = [to_core(p) for s in sums0 for p in cut(s, half)]
    back1 = [to_core(s) for s in sums1]
    parts = [*sums0, *back0, *sums1, *back1, sums2, to_x(sums2)]
    plan = (((0, -1, 1, -2, 2), cuts0, (half,) * 5), ((-3, 3), cuts1, cuts1), ((4,), (), ()))
    wt, rot, proj, there2, there3, near, own = procrustes(
        parts, plan, patient_weights, core, block, masked
    )

    y, z1, z2, z3 = (flip("subj", 8, bit) for bit in (1, 2, 4, 6))
    here2, here3, there0, here0 = term(
        wt, masked, block, ((4,), (6,), (1,), (0,)), (F32, F32, F32, F32)
    )
    got2, own = tie(y(there2), own)
    far2 = z2((here2 + got2.astype(F32)).astype(BF16)).astype(F32)
    got3 = y(there3)
    far3 = z3((here3 + got3.astype(F32)).astype(BF16)).astype(F32)
    other = there0 + z1(near).astype(F32)
    other = jnp.concatenate([y(p) for p in jnp.split(other, 2, axis=0)], 0)
    own = z1(own).astype(F32)
    out = (((here0 + own) + far2) + far3) + other
    rows = patient_rows(rot, proj, npat)
    return out, rows


def per_device_any(visits, tile_pattern, counts, codes_t, core, patient_weights):
    npat = visits.shape[0]
    masked = mask_visits(visits, tile_pattern, counts)
    codes = lax.all_gather(codes_t, "subj", axis=0, tiled=True)
    part = lax.psum(project([codes], masked), "feat")
    wt, rot, proj = procrustes([part], None, patient_weights, core, part.shape[0])
    out = lax.psum_scatter(
        whole_term(wt, masked), "subj", scatter_dimension=0, tiled=True
    )
    return out, patient_rows(rot, proj, npat)


def solution(mesh):
    plan = per_device if (mesh.shape["subj"], mesh.shape["feat"]) == (8, 4) else per_device_any
    return jax.shard_map(
        plan,
        mesh=mesh,
        in_specs=(
            P("subj", None, "feat"),
            P("subj", "feat"),
            P("subj"),
            P("subj", "feat"),
            P(),
            P("subj", None),
        ),
        out_specs=(P("subj", "feat"), P("subj", None)),
        check_vma=False,
    )
```

```python
import functools

import jax
import jax.numpy as jnp
from jax import lax
from jax.experimental import pallas as pl
from jax.experimental.pallas import tpu as pltpu
from jax.sharding import PartitionSpec as P

NS_STEPS = 8
HALF_ROOT = 0.5**0.5
SLOT = 64
BF16, F32 = jnp.bfloat16, jnp.float32
FIRST = ((5,), (7,), (3,), (2,))


def cost(us):
    return pl.CostEstimate(flops=0, bytes_accessed=int(us * 3.6e6), transcendentals=0)

CYCLE = (0, 2, 4, 6, 7, 5, 3, 1)
AHEAD = [(CYCLE[i], CYCLE[(i + 1) % 8]) for i in range(8)]
BACK = [(d, s) for s, d in AHEAD]
NT = (((1,), (1,)), ((), ()))
NN = (((1,), (0,)), ((), ()))


def dot(a, b, dims=NN):
    return lax.dot_general(a, b, dims, preferred_element_type=jnp.float32)


def split2(a):
    hi = a.astype(jnp.bfloat16)
    return hi, (a - hi.astype(jnp.float32)).astype(jnp.bfloat16)


def split3(a):
    hi = a.astype(jnp.bfloat16)
    rest = a - hi.astype(jnp.float32)
    mid = rest.astype(jnp.bfloat16)
    return hi, mid, (rest - mid.astype(jnp.float32)).astype(jnp.bfloat16)


def dot3(a, b, dims=NN):
    ah, al = a
    bh, bl = b
    return dot(ah, bh, dims) + (dot(ah, bl, dims) + dot(al, bh, dims))


def params(mib):
    return pltpu.CompilerParams(vmem_limit_bytes=mib * 1024 * 1024)


def spot(order):
    me = lax.axis_index("subj")
    place = jnp.where(me % 2 == 0, me // 2, 7 - me // 2)
    at = (place + (order + 8)) % 8
    return jnp.where(at < 4, 2 * at, 15 - 2 * at)


def rows_of(index, block):
    return pl.ds(pl.multiple_of(index * block, block), block)


def mask_body(counts_ref, gate_ref, visits_ref, masked_ref):
    k = pl.program_id(0)
    nvis, ncode = visits_ref.shape[1:]
    rows = lax.broadcasted_iota(jnp.int32, (nvis, 1), 0)
    live = (rows < counts_ref[k]).astype(jnp.bfloat16)
    vals = visits_ref[0] * (gate_ref[0] * live)
    masked_ref[...] = jnp.concatenate(
        [vals, jnp.zeros((SLOT - nvis, ncode), jnp.bfloat16)], 0
    )


def mask_visits(visits, tile_pattern, counts):
    npat, nvis, ncode = visits.shape
    gate = jnp.repeat(tile_pattern.astype(jnp.bfloat16), ncode // tile_pattern.shape[1], axis=1)
    return pl.pallas_call(
        mask_body,
        grid=(npat,),
        in_specs=[
            pl.BlockSpec(memory_space=pltpu.SMEM),
            pl.BlockSpec((1, 1, ncode), lambda k: (k, 0, 0)),
            pl.BlockSpec((1, nvis, ncode), lambda k: (k, 0, 0)),
        ],
        out_specs=pl.BlockSpec((SLOT, ncode), lambda k: (k, 0)),
        out_shape=jax.ShapeDtypeStruct((npat * SLOT, ncode), jnp.bfloat16),
        compiler_params=params(4),
        cost_estimate=cost(0),
        name="mask_visits",
    )(counts, gate.reshape(npat, 1, ncode), visits)


def project_body(n, cuts, *refs):
    masked_ref, outs = refs[n], refs[n + 1 :]
    codes = jnp.concatenate([r[...] for r in refs[:n]], 0) if n > 1 else refs[0][...]
    both = dot(codes, masked_ref[...], NT)
    if not cuts:
        outs[0][...] = both
        return
    *outs, whole = outs
    whole[...] = both
    core = lax.axis_index("feat") % 2
    for who, pieces in ((core, outs[: len(cuts)]), (1 - core, outs[len(cuts) :])):
        at = who * sum(cuts)
        for piece, rows in zip(pieces, cuts):
            piece[...] = whole[pl.ds(pl.multiple_of(at, 8), rows), :]
            at = at + rows


def project(blocks, masked, cuts=()):
    rows = sum(b.shape[0] for b in blocks)
    cols = masked.shape[0]
    shapes = [jax.ShapeDtypeStruct((r, cols), F32) for r in (tuple(cuts) * 2 or (rows,))]
    outs = pl.pallas_call(
        functools.partial(project_body, len(blocks), cuts),
        out_shape=shapes,
        scratch_shapes=[pltpu.VMEM((rows, cols), F32)] if cuts else [],
        compiler_params=params(10),
        cost_estimate=cost(0),
        name="project",
    )(*blocks, masked)
    return (outs[: len(cuts)], outs[len(cuts) :]) if cuts else outs[0]


def place_rows(projt, parts, block, plan):
    core = lax.axis_index("feat") % 2
    parts = list(parts)
    for orders, cuts, back in plan:
        if not cuts:
            left, right = parts.pop(0), parts.pop(0)
            for b, order in enumerate(orders):
                rows = slice(b * block, (b + 1) * block)
                projt[rows_of(spot(order), block), :] = left[rows, :] + right[rows, :]
            continue
        half = block // 2
        bases = [spot(o) * 2 + h for o in orders for h in (0, 1)]
        for who, sizes in ((core, cuts), (1 - core, back)):
            at = 0
            for rows in sizes:
                piece = parts.pop(0)
                for u in range(rows // half):
                    base = jnp.where(who == 0, bases[at], bases[len(orders) + at])
                    projt[rows_of(base, half), :] = piece[u * half : (u + 1) * half, :]
                    at += 1


def procrustes_body(block, plan, *refs):
    n = sum(len(cuts) + len(back) or 2 for _, cuts, back in plan) if plan else 1
    parts, (weights_ref, core_ref, *rest) = refs[:n], refs[n:]
    if plan:
        masked_ref, wt_ref, rot_ref, proj_ref, *sends, projt = rest
    else:
        wt_ref, rot_ref, proj_ref, projt = rest
    npat, rank = weights_ref.shape
    if plan:
        place_rows(projt, parts, block, plan)
    else:
        projt[...] = parts[0][...]
    proj = projt[...].T
    proj_ref[...] = proj
    core = core_ref[...]
    weights = weights_ref[...]
    wide = jnp.broadcast_to(weights[:, None, :], (npat, SLOT, rank)).reshape(npat * SLOT, rank)
    hi, lo = split2(proj * wide)
    target = dot(hi, core, NT) + dot(lo, core, NT)
    pair = 2 * SLOT
    row = lax.broadcasted_iota(jnp.int32, (pair, pair), 0) // SLOT
    col = lax.broadcasted_iota(jnp.int32, (pair, pair), 1) // SLOT
    same = row == col
    qs = []
    for p in range(npat // 2):
        two = target[p * pair : (p + 1) * pair].reshape(2, SLOT, rank)
        total = jnp.sum(jnp.sum(two * two, axis=1, keepdims=True), axis=2, keepdims=True)
        qs.append((two * (lax.rsqrt(total + 1e-06) * HALF_ROOT)).reshape(pair, rank))
    for step in range(NS_STEPS):
        halves = [split2(q) for q in qs]
        stacks = [jnp.concatenate(h, 0) for h in halves]
        wides = [dot(k, k, NT) for k in stacks]
        grams = [w[:pair, :pair] + (w[:pair, pair:] + w[pair:, :pair]) for w in wides]
        grams = [split2(jnp.where(same, g, 0.0)) for g in grams]
        prods = [
            dot(jnp.concatenate([g[0], g[0]], 1), k) + dot(g[1], h[0])
            for g, h, k in zip(grams, halves, stacks)
        ]
        qs = [1.5 * q - x for q, x in zip(qs, prods)]
    q = jnp.concatenate(qs, 0)
    hi, lo = split2(q)
    rotated = (dot(hi, core) + dot(lo, core)) * (2.0 * HALF_ROOT)
    rot_ref[...] = rotated
    wt_ref[...] = (rotated * wide).T.astype(jnp.bfloat16)
    if plan:
        term_body(block, FIRST, wt_ref, masked_ref, *sends)


def procrustes(parts, plan, weights, core, block, masked=None):
    npat, rank = weights.shape
    rows = npat * SLOT
    sends = [] if masked is None else [
        jax.ShapeDtypeStruct((len(pick) * block, masked.shape[1]), BF16) for pick in FIRST
    ]
    return pl.pallas_call(
        functools.partial(procrustes_body, block, plan),
        out_shape=[
            jax.ShapeDtypeStruct((rank, rows), jnp.bfloat16),
            jax.ShapeDtypeStruct((rows, rank), jnp.float32),
            jax.ShapeDtypeStruct((rows, rank), jnp.float32),
            *sends,
        ],
        scratch_shapes=[pltpu.VMEM((rank, rows), jnp.float32)],
        compiler_params=params(16),
        cost_estimate=cost(4.8),
        name="procrustes",
    )(*parts, weights, core, *([] if masked is None else [masked]))


def rows_body(rot_ref, proj_ref, out_ref):
    npat, rank = out_ref.shape
    prod = rot_ref[...] * proj_ref[...]
    out_ref[...] = jnp.sum(prod.reshape(npat, SLOT, rank), axis=1)


def patient_rows(rot, proj, npat):
    return pl.pallas_call(
        rows_body,
        out_shape=jax.ShapeDtypeStruct((npat, rot.shape[1]), jnp.float32),
        compiler_params=params(4),
        name="patient_rows",
    )(rot, proj)


def term_body(block, picks, wt_ref, masked_ref, *out_refs):
    me = lax.axis_index("subj")
    flips = [f for pick in picks for f in pick]
    wt = jnp.concatenate([wt_ref[rows_of(me ^ f, block), :] for f in flips], 0)
    both = dot(wt, masked_ref[...])
    at = 0
    for out_ref in out_refs:
        rows = out_ref.shape[0]
        out_ref[...] = both[at : at + rows].astype(out_ref.dtype)
        at += rows


def term(wt, masked, block, picks, kinds):
    ncode = masked.shape[1]
    rows = [len(pick) * block for pick in picks]
    return pl.pallas_call(
        functools.partial(term_body, block, picks),
        out_shape=[jax.ShapeDtypeStruct((r, ncode), kind) for r, kind in zip(rows, kinds)],
        compiler_params=params(10),
        cost_estimate=cost(0),
        name="term",
    )(wt, masked)


def whole_term_body(wt_ref, masked_ref, out_ref):
    out_ref[...] = dot(wt_ref[...], masked_ref[...])


def whole_term(wt, masked):
    return pl.pallas_call(
        whole_term_body,
        out_shape=jax.ShapeDtypeStruct((wt.shape[0], masked.shape[1]), jnp.float32),
        compiler_params=params(16),
        name="whole_term",
    )(wt, masked)


def flip(axis, size, bit):
    return functools.partial(
        lax.ppermute, axis_name=axis, perm=[(s, s ^ bit) for s in range(size)]
    )


def tie(first, then):
    return lax.optimization_barrier((first, then))


def cut(a, rows):
    return jnp.split(a, a.shape[0] // rows, axis=0)


def per_device(visits, tile_pattern, counts, codes_t, core, patient_weights):
    npat = visits.shape[0]
    block = codes_t.shape[0]
    half = block // 2
    to_core, to_x = flip("feat", 4, 1), flip("feat", 4, 2)

    def step(ahead, back):
        return lax.ppermute(ahead, "subj", AHEAD), lax.ppermute(back, "subj", BACK)

    masked = mask_visits(visits, tile_pattern, counts)
    one = step(codes_t, codes_t)
    two = step(*one)
    masked, back = tie(masked, two[1])
    two = (two[0], back)
    three = step(*two)
    four = (lax.ppermute(three[1], "subj", BACK),)
    cuts0 = (5 * half,)
    sums0 = [m + to_core(t) for m, t in zip(*project([codes_t, *one, *two], masked, cuts0))]
    from0 = [to_x(s) for s in sums0]
    cuts1 = (2 * half,)
    sums1 = [m + to_core(t) for m, t in zip(*project([*three], masked, cuts1))]
    from1 = [to_x(s) for s in sums1]
    sums2 = project([*four], masked)
    sums2 = sums2 + to_core(sums2)
    sums2, from1 = tie(sums2, from1)
    sums0 = [s + f for s, f in zip(sums0, from0)]
    sums1 = [s + f for s, f in zip(sums1, from1)]
    back0 = [to_core(p) for s in sums0 for p in cut(s, half)]
    back1 = [to_core(s) for s in sums1]
    parts = [*sums0, *back0, *sums1, *back1, sums2, to_x(sums2)]
    plan = (((0, -1, 1, -2, 2), cuts0, (half,) * 5), ((-3, 3), cuts1, cuts1), ((4,), (), ()))
    wt, rot, proj, there2, there3, near, own = procrustes(
        parts, plan, patient_weights, core, block, masked
    )

    y, z1, z2, z3 = (flip("subj", 8, bit) for bit in (1, 2, 4, 6))
    here2, here3, there0, here0 = term(
        wt, masked, block, ((4,), (6,), (1,), (0,)), (F32, F32, F32, F32)
    )
    got2, own = tie(y(there2), own)
    far2 = z2((here2 + got2.astype(F32)).astype(BF16)).astype(F32)
    got3 = y(there3)
    far3 = z3((here3 + got3.astype(F32)).astype(BF16)).astype(F32)
    other = there0 + z1(near).astype(F32)
    other = y(other)
    own = z1(own).astype(F32)
    out = (((here0 + own) + far2) + far3) + other
    rows = patient_rows(rot, proj, npat)
    return out, rows


def per_device_any(visits, tile_pattern, counts, codes_t, core, patient_weights):
    npat = visits.shape[0]
    masked = mask_visits(visits, tile_pattern, counts)
    codes = lax.all_gather(codes_t, "subj", axis=0, tiled=True)
    part = lax.psum(project([codes], masked), "feat")
    wt, rot, proj = procrustes([part], None, patient_weights, core, part.shape[0])
    out = lax.psum_scatter(
        whole_term(wt, masked), "subj", scatter_dimension=0, tiled=True
    )
    return out, patient_rows(rot, proj, npat)


def solution(mesh):
    plan = per_device if (mesh.shape["subj"], mesh.shape["feat"]) == (8, 4) else per_device_any
    return jax.shard_map(
        plan,
        mesh=mesh,
        in_specs=(
            P("subj", None, "feat"),
            P("subj", "feat"),
            P("subj"),
            P("subj", "feat"),
            P(),
            P("subj", None),
        ),
        out_specs=(P("subj", "feat"), P("subj", None)),
        check_vma=False,
    )
```

```python
import functools

import jax
import jax.numpy as jnp
from jax import lax
from jax.experimental import pallas as pl
from jax.experimental.pallas import tpu as pltpu
from jax.sharding import PartitionSpec as P

NS_STEPS = 8
SLOT = 64
BF16, F32 = jnp.bfloat16, jnp.float32
FIRST = ((5,), (7,), (3,), (2,))


def cost(us):
    return pl.CostEstimate(flops=0, bytes_accessed=int(us * 3.6e6), transcendentals=0)

CYCLE = (0, 2, 4, 6, 7, 5, 3, 1)
AHEAD = [(CYCLE[i], CYCLE[(i + 1) % 8]) for i in range(8)]
BACK = [(d, s) for s, d in AHEAD]
NT = (((1,), (1,)), ((), ()))
NN = (((1,), (0,)), ((), ()))


def dot(a, b, dims=NN):
    return lax.dot_general(a, b, dims, preferred_element_type=jnp.float32)


def split2(a):
    hi = a.astype(jnp.bfloat16)
    return hi, (a - hi.astype(jnp.float32)).astype(jnp.bfloat16)


def split3(a):
    hi = a.astype(jnp.bfloat16)
    rest = a - hi.astype(jnp.float32)
    mid = rest.astype(jnp.bfloat16)
    return hi, mid, (rest - mid.astype(jnp.float32)).astype(jnp.bfloat16)


def dot3(a, b, dims=NN):
    ah, al = a
    bh, bl = b
    return dot(ah, bh, dims) + (dot(ah, bl, dims) + dot(al, bh, dims))


def params(mib):
    return pltpu.CompilerParams(vmem_limit_bytes=mib * 1024 * 1024)


def spot(order):
    me = lax.axis_index("subj")
    place = jnp.where(me % 2 == 0, me // 2, 7 - me // 2)
    at = (place + (order + 8)) % 8
    return jnp.where(at < 4, 2 * at, 15 - 2 * at)


def rows_of(index, block):
    return pl.ds(pl.multiple_of(index * block, block), block)


def mask_body(counts_ref, gate_ref, visits_ref, masked_ref):
    k = pl.program_id(0)
    nvis, ncode = visits_ref.shape[1:]
    rows = lax.broadcasted_iota(jnp.int32, (nvis, 1), 0)
    live = (rows < counts_ref[k]).astype(jnp.bfloat16)
    vals = visits_ref[0] * (gate_ref[0] * live)
    masked_ref[...] = jnp.concatenate(
        [vals, jnp.zeros((SLOT - nvis, ncode), jnp.bfloat16)], 0
    )


def mask_visits(visits, tile_pattern, counts):
    npat, nvis, ncode = visits.shape
    gate = jnp.repeat(tile_pattern.astype(jnp.bfloat16), ncode // tile_pattern.shape[1], axis=1)
    return pl.pallas_call(
        mask_body,
        grid=(npat,),
        in_specs=[
            pl.BlockSpec(memory_space=pltpu.SMEM),
            pl.BlockSpec((1, 1, ncode), lambda k: (k, 0, 0)),
            pl.BlockSpec((1, nvis, ncode), lambda k: (k, 0, 0)),
        ],
        out_specs=pl.BlockSpec((SLOT, ncode), lambda k: (k, 0)),
        out_shape=jax.ShapeDtypeStruct((npat * SLOT, ncode), jnp.bfloat16),
        compiler_params=params(4),
        cost_estimate=cost(0),
        name="mask_visits",
    )(counts, gate.reshape(npat, 1, ncode), visits)


def project_body(n, cuts, *refs):
    masked_ref, outs = refs[n], refs[n + 1 :]
    codes = jnp.concatenate([r[...] for r in refs[:n]], 0) if n > 1 else refs[0][...]
    both = dot(codes, masked_ref[...], NT)
    if not cuts:
        outs[0][...] = both
        return
    *outs, whole = outs
    whole[...] = both
    core = lax.axis_index("feat") % 2
    for who, pieces in ((core, outs[: len(cuts)]), (1 - core, outs[len(cuts) :])):
        at = who * sum(cuts)
        for piece, rows in zip(pieces, cuts):
            piece[...] = whole[pl.ds(pl.multiple_of(at, 8), rows), :]
            at = at + rows


def project(blocks, masked, cuts=()):
    rows = sum(b.shape[0] for b in blocks)
    cols = masked.shape[0]
    shapes = [jax.ShapeDtypeStruct((r, cols), F32) for r in (tuple(cuts) * 2 or (rows,))]
    outs = pl.pallas_call(
        functools.partial(project_body, len(blocks), cuts),
        out_shape=shapes,
        scratch_shapes=[pltpu.VMEM((rows, cols), F32)] if cuts else [],
        compiler_params=params(10),
        cost_estimate=cost(0),
        name="project",
    )(*blocks, masked)
    return (outs[: len(cuts)], outs[len(cuts) :]) if cuts else outs[0]


def place_rows(projt, parts, block, plan):
    core = lax.axis_index("feat") % 2
    parts = list(parts)
    for orders, cuts, back in plan:
        if not cuts:
            left, right = parts.pop(0), parts.pop(0)
            for b, order in enumerate(orders):
                rows = slice(b * block, (b + 1) * block)
                projt[rows_of(spot(order), block), :] = left[rows, :] + right[rows, :]
            continue
        half = block // 2
        bases = [spot(o) * 2 + h for o in orders for h in (0, 1)]
        for who, sizes in ((core, cuts), (1 - core, back)):
            at = 0
            for rows in sizes:
                piece = parts.pop(0)
                for u in range(rows // half):
                    base = jnp.where(who == 0, bases[at], bases[len(orders) + at])
                    projt[rows_of(base, half), :] = piece[u * half : (u + 1) * half, :]
                    at += 1


def procrustes_body(block, plan, *refs):
    n = sum(len(cuts) + len(back) or 2 for _, cuts, back in plan) if plan else 1
    parts, (weights_ref, core_ref, *rest) = refs[:n], refs[n:]
    if plan:
        masked_ref, wt_ref, rot_ref, proj_ref, *sends, projt = rest
    else:
        wt_ref, rot_ref, proj_ref, projt = rest
    npat, rank = weights_ref.shape
    if plan:
        place_rows(projt, parts, block, plan)
    else:
        projt[...] = parts[0][...]
    proj = projt[...].T
    proj_ref[...] = proj
    core = core_ref[...]
    weights = weights_ref[...]
    wide = jnp.broadcast_to(weights[:, None, :], (npat, SLOT, rank)).reshape(npat * SLOT, rank)
    hi, lo = split2(proj * wide)
    target = dot(hi, core, NT) + dot(lo, core, NT)
    pair = 2 * SLOT
    row = lax.broadcasted_iota(jnp.int32, (pair, pair), 0) // SLOT
    col = lax.broadcasted_iota(jnp.int32, (pair, pair), 1) // SLOT
    same = row == col
    qs = []
    for p in range(npat // 2):
        two = target[p * pair : (p + 1) * pair].reshape(2, SLOT, rank)
        total = jnp.sum(jnp.sum(two * two, axis=1, keepdims=True), axis=2, keepdims=True)
        qs.append((two * lax.rsqrt(total + 1e-06)).reshape(pair, rank))
    for step in range(NS_STEPS):
        halves = [split2(q) for q in qs]
        stacks = [jnp.concatenate(h, 0) for h in halves]
        wides = [dot(k, k, NT) for k in stacks]
        grams = [w[:pair, :pair] + (w[:pair, pair:] + w[pair:, :pair]) for w in wides]
        grams = [split2(jnp.where(same, g, 0.0)) for g in grams]
        prods = [
            dot(jnp.concatenate([g[0], g[0]], 1), k) + dot(g[1], h[0])
            for g, h, k in zip(grams, halves, stacks)
        ]
        qs = [1.5 * q - 0.5 * x for q, x in zip(qs, prods)]
    q = jnp.concatenate(qs, 0)
    hi, lo = split2(q)
    rotated = dot(hi, core) + dot(lo, core)
    rot_ref[...] = rotated
    wt_ref[...] = (rotated * wide).T.astype(jnp.bfloat16)
    if plan:
        term_body(block, FIRST, wt_ref, masked_ref, *sends)


def procrustes(parts, plan, weights, core, block, masked=None):
    npat, rank = weights.shape
    rows = npat * SLOT
    sends = [] if masked is None else [
        jax.ShapeDtypeStruct((len(pick) * block, masked.shape[1]), BF16) for pick in FIRST
    ]
    return pl.pallas_call(
        functools.partial(procrustes_body, block, plan),
        out_shape=[
            jax.ShapeDtypeStruct((rank, rows), jnp.bfloat16),
            jax.ShapeDtypeStruct((rows, rank), jnp.float32),
            jax.ShapeDtypeStruct((rows, rank), jnp.float32),
            *sends,
        ],
        scratch_shapes=[pltpu.VMEM((rank, rows), jnp.float32)],
        compiler_params=params(16),
        cost_estimate=cost(4.8),
        name="procrustes",
    )(*parts, weights, core, *([] if masked is None else [masked]))


def rows_body(rot_ref, proj_ref, out_ref):
    npat, rank = out_ref.shape
    prod = rot_ref[...] * proj_ref[...]
    out_ref[...] = jnp.sum(prod.reshape(npat, SLOT, rank), axis=1)


def patient_rows(rot, proj, npat):
    return pl.pallas_call(
        rows_body,
        out_shape=jax.ShapeDtypeStruct((npat, rot.shape[1]), jnp.float32),
        compiler_params=params(4),
        name="patient_rows",
    )(rot, proj)


def term_body(block, picks, wt_ref, masked_ref, *out_refs):
    me = lax.axis_index("subj")
    flips = [f for pick in picks for f in pick]
    wt = jnp.concatenate([wt_ref[rows_of(me ^ f, block), :] for f in flips], 0)
    both = dot(wt, masked_ref[...])
    at = 0
    for out_ref in out_refs:
        rows = out_ref.shape[0]
        out_ref[...] = both[at : at + rows].astype(out_ref.dtype)
        at += rows


def term(wt, masked, block, picks, kinds):
    ncode = masked.shape[1]
    rows = [len(pick) * block for pick in picks]
    return pl.pallas_call(
        functools.partial(term_body, block, picks),
        out_shape=[jax.ShapeDtypeStruct((r, ncode), kind) for r, kind in zip(rows, kinds)],
        compiler_params=params(10),
        cost_estimate=cost(0),
        name="term",
    )(wt, masked)


def whole_term_body(wt_ref, masked_ref, out_ref):
    out_ref[...] = dot(wt_ref[...], masked_ref[...])


def whole_term(wt, masked):
    return pl.pallas_call(
        whole_term_body,
        out_shape=jax.ShapeDtypeStruct((wt.shape[0], masked.shape[1]), jnp.float32),
        compiler_params=params(16),
        name="whole_term",
    )(wt, masked)


def flip(axis, size, bit):
    return functools.partial(
        lax.ppermute, axis_name=axis, perm=[(s, s ^ bit) for s in range(size)]
    )


def tie(first, then):
    return lax.optimization_barrier((first, then))


def cut(a, rows):
    return jnp.split(a, a.shape[0] // rows, axis=0)


def per_device(visits, tile_pattern, counts, codes_t, core, patient_weights):
    npat = visits.shape[0]
    block = codes_t.shape[0]
    half = block // 2
    to_core, to_x = flip("feat", 4, 1), flip("feat", 4, 2)

    def step(ahead, back):
        return lax.ppermute(ahead, "subj", AHEAD), lax.ppermute(back, "subj", BACK)

    masked = mask_visits(visits, tile_pattern, counts)
    one = step(codes_t, codes_t)
    masked, back = tie(masked, one[1])
    one = (one[0], back)
    two = step(*one)
    three = step(*two)
    four = (lax.ppermute(three[1], "subj", BACK),)
    cuts0 = (5 * half,)
    sums0 = [m + to_core(t) for m, t in zip(*project([codes_t, *one, *two], masked, cuts0))]
    from0 = [to_x(s) for s in sums0]
    cuts1 = (2 * half,)
    sums1 = [m + to_core(t) for m, t in zip(*project([*three], masked, cuts1))]
    from1 = [to_x(s) for s in sums1]
    sums2 = project([*four], masked)
    sums2 = sums2 + to_core(sums2)
    sums2, from1 = tie(sums2, from1)
    sums0 = [s + f for s, f in zip(sums0, from0)]
    sums1 = [s + f for s, f in zip(sums1, from1)]
    back0 = [to_core(p) for s in sums0 for p in cut(s, half)]
    back1 = [to_core(p) for s in sums1 for p in cut(s, half)]
    parts = [*sums0, *back0, *sums1, *back1, sums2, to_x(sums2)]
    plan = (((0, -1, 1, -2, 2), cuts0, (half,) * 5), ((-3, 3), cuts1, (half,) * 2), ((4,), (), ()))
    wt, rot, proj, there2, there3, near, own = procrustes(
        parts, plan, patient_weights, core, block, masked
    )

    y, z1, z2, z3 = (flip("subj", 8, bit) for bit in (1, 2, 4, 6))
    here2, here3, there0, here0 = term(
        wt, masked, block, ((4,), (6,), (1,), (0,)), (F32, F32, F32, F32)
    )
    got2, own = tie(y(there2), own)
    far2 = z2((here2 + got2.astype(F32)).astype(BF16)).astype(F32)
    got3 = y(there3)
    far3 = z3((here3 + got3.astype(F32)).astype(BF16)).astype(F32)
    other = there0 + z1(near).astype(F32)
    other = jnp.concatenate([y(p) for p in jnp.split(other, 2, axis=0)], 0)
    own = z1(own).astype(F32)
    out = (((here0 + own) + far2) + far3) + other
    rows = patient_rows(rot, proj, npat)
    return out, rows


def per_device_any(visits, tile_pattern, counts, codes_t, core, patient_weights):
    npat = visits.shape[0]
    masked = mask_visits(visits, tile_pattern, counts)
    codes = lax.all_gather(codes_t, "subj", axis=0, tiled=True)
    part = lax.psum(project([codes], masked), "feat")
    wt, rot, proj = procrustes([part], None, patient_weights, core, part.shape[0])
    out = lax.psum_scatter(
        whole_term(wt, masked), "subj", scatter_dimension=0, tiled=True
    )
    return out, patient_rows(rot, proj, npat)


def solution(mesh):
    plan = per_device if (mesh.shape["subj"], mesh.shape["feat"]) == (8, 4) else per_device_any
    return jax.shard_map(
        plan,
        mesh=mesh,
        in_specs=(
            P("subj", None, "feat"),
            P("subj", "feat"),
            P("subj"),
            P("subj", "feat"),
            P(),
            P("subj", None),
        ),
        out_specs=(P("subj", "feat"), P("subj", None)),
        check_vma=False,
    )
```
